128 devices in a mesh: grp: 4 (over x), dev: 32 (over z, y, core).
Axes of the slice: x: 4, y: 4, z: 4, core: 2. Of those that a mesh axis runs over, the one named last changes fastest.
Arguments:
- populations: float32 [512, 19, 4096], P(('grp', 'dev')), may hold values from 0.02 to 2.1
- solidity: float32 [512, 4096], P(('grp', 'dev')), may hold values from 0 to 1
- home_count: int32 [4, 8, 4], P('grp'), may hold values from 1 to 4, 8 in all within a row
Outputs:
- evolved: float32 [256, 19, 4096], P(('grp', 'dev'))
The draws below stay inside these ranges and needn't reach their ends.
Inputs may be any that keep to these rules, and one draw needn't show every extreme that they name: `home_count`: each row of 4 counts sums to 8.
All inputs are finite; a program needn't handle non-finite values.
Results may differ from the reference program's by a relative error of at most 0.0001.
Values sent between devices are 32-bit elements; how exact they have to be, the bound alone decides.
A program may use at most 64 MiB of HBM per device.

```python
import math
import jax
import jax.numpy as jnp
import numpy as np
from jax import lax

B = 16
AVG = 2
HS = 4
TEAM = 4
Q = 19
STEPS = 2
C = 4096
NX = 64
NZ = 1024
TEAMS = 8
SLOTS = 512
BLOCKS = 256
N_GRP = 4
N_DEV = 32


def lattice_weights():
    return jnp.array([1.0 / 3.0] + [1.0 / 18.0] * 6 + [1.0 / 36.0] * 12, jnp.float32)


def draw_populations(key, part):
    key = jax.random.fold_in(key, 11)
    jitter_key = jax.random.fold_in(key, 0)
    weights = lattice_weights()
    jitter = jax.random.normal(jitter_key, (SLOTS, Q, C), jnp.float32)
    values = 1.0 + 0.3 * jnp.clip(jitter, -2.0, 2.0)
    return (3.0 * weights[None, :, None] * values).astype(jnp.float32)


def draw_solidity(key, part):
    key = jax.random.fold_in(key, 23)
    level_key, cell_key, gray_key = jax.random.split(key, 3)
    density = jax.random.uniform(level_key, (SLOTS, 1), jnp.float32, 0.1, 0.5)
    chance = jax.random.uniform(cell_key, (SLOTS, C), jnp.float32)
    grayness = jax.random.uniform(gray_key, (SLOTS, C), jnp.float32)
    return jnp.where(chance < density, 1.0, jnp.where(chance < density + 0.3, grayness, 0.0)).astype(jnp.float32)


def length_profile(count, total, reach, skew):
    portions = [(1 << 20) // math.isqrt(rank ** skew) + 1 for rank in range(2, count + 1)]
    spare, given = total - reach - (count - 1), [1] * (count - 1)
    while spare > 0:
        candidates = [i for i in range(count - 1) if given[i] < reach]
        mass, remaining = sum([portions[i] for i in candidates]), spare
        for i in candidates:
            more = min(reach - given[i], max(1, remaining * portions[i] // mass), spare)
            given[i] = given[i] + more
            spare = spare - more
    return np.array([reach] + given)


def uneven(rng, number_of, total, most, skew):
    if number_of == 2:
        one = jax.random.randint(rng, (), max(1, total - most), min(most, total - 1) + 1)
        return jnp.stack([one, total - one])
    lengths = jnp.asarray(length_profile(number_of, total, most, skew), jnp.int32)
    couples = (number_of - 1) // 2
    source_of, sink = lengths[1:1 + 2 * couples:2], lengths[2:2 + 2 * couples:2]
    margin = jnp.minimum(source_of - 1, most - sink)
    passed = jax.random.randint(jax.random.fold_in(rng, 1), (couples,), 0, 1 << 20) % (margin + 1)
    lengths = lengths.at[1:1 + 2 * couples:2].set(source_of - passed).at[2:2 + 2 * couples:2].set(sink + passed)
    return lengths[jax.random.permutation(jax.random.fold_in(rng, 2), number_of)]


def setup_inputs(seed: int = 0) -> dict:
    keys = jax.random.split(jax.random.key(seed), 4)
    return {
        "populations": draw_populations(jax.random.fold_in(keys[3], 71), 0),
        "solidity": draw_solidity(jax.random.fold_in(keys[3], 71), 0),
        "home_count": jax.vmap(lambda own: uneven(own, TEAM, TEAM * AVG, HS, 2))(jax.random.split(keys[2], N_GRP * TEAMS)).reshape((N_GRP, TEAMS, TEAM)).astype(jnp.int32),
    }


speeds = np.array([[0, 0, 0], [1, 0, 0], [-1, 0, 0], [0, 1, 0], [0, -1, 0], [0, 0, 1], [0, 0, -1], [1, 1, 0], [-1, -1, 0], [1, -1, 0], [-1, 1, 0], [1, 0, 1], [-1, 0, -1], [1, 0, -1], [-1, 0, 1], [0, 1, 1], [0, -1, -1], [0, 1, -1], [0, -1, 1]])
mirror = [0, 2, 1, 4, 3, 6, 5, 8, 7, 10, 9, 12, 11, 14, 13, 16, 15, 18, 17]
relax_rates = [0.0, 1.19, 1.4, 0.0, 1.2, 0.0, 1.2, 0.0, 1.2, 1.25, 1.4, 1.25, 1.4, 1.25, 1.25, 1.25, 1.98, 1.98, 1.98]
rest_density = 3.0


def moment_table():
    along_x = speeds[:, 0] * 1.0
    along_y = speeds[:, 1] * 1.0
    along_z = speeds[:, 2] * 1.0
    squared = along_x * along_x + along_y * along_y + along_z * along_z
    moment_rows = [np.ones(19), 19 * squared - 30, (21 * squared * squared - 53 * squared + 24) / 2,
                   along_x, (5 * squared - 9) * along_x, along_y, (5 * squared - 9) * along_y,
                   along_z, (5 * squared - 9) * along_z, 3 * along_x * along_x - squared,
                   (3 * squared - 5) * (3 * along_x * along_x - squared), along_y * along_y - along_z * along_z,
                   (3 * squared - 5) * (along_y * along_y - along_z * along_z), along_x * along_y,
                   along_y * along_z, along_x * along_z, (along_y * along_y - along_z * along_z) * along_x,
                   (along_z * along_z - along_x * along_x) * along_y, (along_x * along_x - along_y * along_y) * along_z]
    forward = np.stack(moment_rows)
    inverse = forward.T / np.sum(forward * forward, axis=1)[None, :]
    return jnp.asarray(forward, jnp.float32), jnp.asarray(inverse, jnp.float32)


def collide(field, solid_part):
    forward, inverse = moment_table()
    flat_cells = field.reshape(19, -1)
    moments = jnp.dot(forward, flat_cells, precision=lax.Precision.HIGHEST, preferred_element_type=jnp.float32)
    density = moments[0]
    flux_x = moments[3]
    flux_y = moments[5]
    flux_z = moments[7]
    square = flux_x * flux_x + flux_y * flux_y + flux_z * flux_z
    stress_xx = (3.0 * flux_x * flux_x - square) / rest_density
    stress_ww = (flux_y * flux_y - flux_z * flux_z) / rest_density
    nothing = jnp.zeros_like(density)
    balance = jnp.stack([density, -11.0 * density + 19.0 * square / rest_density,
                         3.0 * density - 5.5 * square / rest_density,
                         flux_x, -2.0 / 3.0 * flux_x, flux_y, -2.0 / 3.0 * flux_y, flux_z, -2.0 / 3.0 * flux_z,
                         stress_xx, -0.5 * stress_xx, stress_ww, -0.5 * stress_ww,
                         flux_x * flux_y / rest_density, flux_y * flux_z / rest_density,
                         flux_x * flux_z / rest_density, nothing, nothing, nothing])
    relax_table = jnp.asarray(np.array(relax_rates), jnp.float32)[:, None]
    relaxed = moments - relax_table * (moments - balance)
    collided = jnp.dot(inverse, relaxed, precision=lax.Precision.HIGHEST, preferred_element_type=jnp.float32)
    collided = collided.reshape(field.shape)
    solid_share = solid_part[None]
    return (1.0 - solid_share) * collided + solid_share * field[np.array(mirror)]


def home_slots(home_count):
    inclusive = jnp.cumsum(home_count, axis=2).astype(jnp.int32)
    starts = (inclusive - home_count).astype(jnp.int32)
    blocks = jnp.arange(NZ // B, dtype=jnp.int32)
    team_index = blocks // (TEAM * AVG)
    within = blocks % (TEAM * AVG)
    team_inclusive = inclusive[:, team_index, :]
    member = jnp.sum((team_inclusive <= within[None, :, None]).astype(jnp.int32), axis=2)
    team_starts = starts[:, team_index, :]
    start_member = jnp.take_along_axis(team_starts, member[:, :, None], axis=2)[:, :, 0]
    offset = within[None, :] - start_member
    groups = jnp.arange(N_GRP, dtype=jnp.int32)[:, None]
    return ((groups * N_DEV + team_index[None, :] * TEAM + member) * HS + offset).astype(jnp.int32)


def reference(populations, solidity, home_count):
    slot_list = home_slots(home_count).reshape(-1)
    column_blocks = NZ // B
    picked = populations[slot_list].reshape(N_GRP, column_blocks, Q, B, B, B)
    lattice = picked.transpose(0, 3, 2, 4, 1, 5).reshape(NX, Q, B, NZ)
    solid_pick = solidity[slot_list].reshape(N_GRP, column_blocks, B, B, B)
    solid_part = solid_pick.transpose(0, 2, 3, 1, 4).reshape(NX, B, NZ)
    for repeat in range(STEPS):
        collided = lax.map(lambda pair: collide(pair[0], pair[1]), (lattice, solid_part))
        shifted = []
        for direction in range(19):
            moves = (int(speeds[direction, 0]), int(speeds[direction, 1]), int(speeds[direction, 2]))
            shifted.append(jnp.roll(collided[:, direction], moves, axis=(0, 1, 2)))
        lattice = jnp.stack(shifted, axis=1)
    blocked = lattice.reshape(N_GRP, B, Q, B, column_blocks, B).transpose(0, 4, 2, 1, 3, 5)
    return blocked.reshape(BLOCKS, Q, C)
```

```python
import jax
import jax.numpy as jnp
import numpy as np
from jax import lax
from jax.experimental import pallas as pl
from jax.experimental.pallas import tpu as pltpu
from jax.sharding import PartitionSpec as P

MESH = pl.DeviceIdType.MESH
B = 16
AVG = 2
HS = 4
TEAM = 4
Q = 19
C = B * B * B
LANES = 128
TILES = C // LANES
CHUNKS = 2
PER_CHUNK = TILES // CHUNKS
CELL_ROWS = PER_CHUNK * Q
CHUNK_ROWS = CELL_ROWS + PER_CHUNK
MAIN = 8
ROWS = 32
NEXT_ROWS = 24

SPEEDS = [
    (0, 0, 0), (1, 0, 0), (-1, 0, 0), (0, 1, 0), (0, -1, 0), (0, 0, 1), (0, 0, -1), (1, 1, 0), (-1, -1, 0), (1, -1, 0),
    (-1, 1, 0), (1, 0, 1), (-1, 0, -1), (1, 0, -1), (-1, 0, 1), (0, 1, 1), (0, -1, -1), (0, 1, -1), (0, -1, 1),
]
SOLID = Q
ORDER = (
    [d for d in range(Q) if SPEEDS[d][0] == 1]
    + [SOLID]
    + [d for d in range(Q) if SPEEDS[d][0] == 0]
    + [d for d in range(Q) if SPEEDS[d][0] == -1]
)
SLOT = {d: place for place, d in enumerate(ORDER)}
SLOTS = Q + 1
FORWARD = 15

UP_FACE = [
    [(d, 15) for d in range(Q) if SPEEDS[d][2] >= 0] + [(SOLID, 15)],
    [(d, 14) for d in range(Q) if SPEEDS[d][2] == 1],
]
DOWN_FACE = [
    [(d, 0) for d in range(Q) if SPEEDS[d][2] <= 0] + [(SOLID, 0)],
    [(d, 1) for d in range(Q) if SPEEDS[d][2] == -1],
]


def rolled(value, amount):
    amount %= LANES
    return pltpu.roll(value, amount, 1) if amount else value


def collide(f, n):
    pair = {}
    gap = {}
    for i in range(1, Q, 2):
        pair[i] = f[i] + f[i + 1]
        gap[i] = f[i] - f[i + 1]
    xy, xz, yz = pair[7] + pair[9], pair[11] + pair[13], pair[15] + pair[17]
    axes_yz = pair[3] + pair[5]
    axes = pair[1] + axes_yz
    xy_xz = xy + xz
    diagonals = xy_xz + yz
    rho = f[0] + axes + diagonals
    energy = 8.0 * diagonals - 11.0 * axes - 30.0 * f[0]
    energy_2 = diagonals - 4.0 * axes + 12.0 * f[0]
    axial = 2.0 * pair[1] - axes_yz
    planar = xy_xz - 2.0 * yz
    axial_w = pair[3] - pair[5]
    planar_w = xy - xz
    gx_xy, gx_xz = gap[7] + gap[9], gap[11] + gap[13]
    gy_xy, gy_yz = gap[7] - gap[9], gap[15] + gap[17]
    gz_xz, gz_yz = gap[11] - gap[13], gap[15] - gap[17]
    dx, dy, dz = gx_xy + gx_xz, gy_xy + gy_yz, gz_xz + gz_yz
    jx, jy, jz = gap[1] + dx, gap[3] + dy, gap[5] + dz
    third = 1.0 / 3.0
    xx, yy, zz = jx * jx, jy * jy, jz * jz
    yyzz = yy + zz
    square = xx + yyzz
    p = (2.0 * third) * xx - third * yyzz
    w = third * (yy - zz)
    open_share = 1.0 - n

    def relaxed(rate, norm, excess):
        return (rate / norm) * excess

    r_e = open_share * relaxed(1.19, 2394.0, energy + 11.0 * rho - (19.0 * third) * square)
    r_e2 = open_share * relaxed(1.4, 252.0, energy_2 - 3.0 * rho + (5.5 * third) * square)
    r_p = open_share * relaxed(1.25, 36.0, axial + planar - p)
    r_p2 = open_share * relaxed(1.4, 72.0, planar - 2.0 * axial + 0.5 * p)
    r_w = open_share * relaxed(1.25, 12.0, axial_w + planar_w - w)
    r_w2 = open_share * relaxed(1.4, 24.0, planar_w - 2.0 * axial_w + 0.5 * w)
    third_j = (third * jx, third * jy)
    r_xy = open_share * relaxed(1.25, 4.0, pair[7] - pair[9] - third_j[0] * jy)
    r_yz = open_share * relaxed(1.25, 4.0, pair[15] - pair[17] - third_j[1] * jz)
    r_xz = open_share * relaxed(1.25, 4.0, pair[11] - pair[13] - third_j[0] * jz)
    r_qx = open_share * relaxed(1.2, 40.0, dx - 4.0 * gap[1] + (2.0 * third) * jx)
    r_qy = open_share * relaxed(1.2, 40.0, dy - 4.0 * gap[3] + (2.0 * third) * jy)
    r_qz = open_share * relaxed(1.2, 40.0, dz - 4.0 * gap[5] + (2.0 * third) * jz)
    r_mx = open_share * relaxed(1.98, 8.0, gx_xy - gx_xz)
    r_my = open_share * relaxed(1.98, 8.0, gy_yz - gy_xy)
    r_mz = open_share * relaxed(1.98, 8.0, gz_xz - gz_yz)

    even_axis = -11.0 * r_e - 4.0 * r_e2
    even_plane = 8.0 * r_e + r_e2
    a_p = r_p - 2.0 * r_p2
    a_w = r_w - 2.0 * r_w2
    d_p = r_p + r_p2
    d_w = r_w + r_w2
    axis_rest = even_axis - a_p
    plane_x = even_plane + d_p
    even_xy, even_xz, even_yz = plane_x + d_w, plane_x - d_w, even_plane - 2.0 * d_p
    x_plus, x_minus = r_qx + r_mx, r_qx - r_mx
    y_plus, y_minus = r_qy + r_my, r_qy - r_my
    z_plus, z_minus = r_qz + r_mz, r_qz - r_mz
    even = {
        1: even_axis + 2.0 * a_p,
        3: axis_rest + a_w,
        5: axis_rest - a_w,
        7: even_xy + r_xy,
        9: even_xy - r_xy,
        11: even_xz + r_xz,
        13: even_xz - r_xz,
        15: even_yz + r_yz,
        17: even_yz - r_yz,
    }
    odd = {
        1: -4.0 * r_qx,
        3: -4.0 * r_qy,
        5: -4.0 * r_qz,
        7: x_plus + y_minus,
        9: x_plus - y_minus,
        11: x_minus + z_plus,
        13: x_minus - z_plus,
        15: y_plus + z_minus,
        17: y_plus - z_minus,
    }
    post = [f[0] - (12.0 * r_e2 - 30.0 * r_e)]
    for i in range(1, Q, 2):
        turned = n * gap[i] + odd[i]
        post.append(f[i] - even[i] - turned)
        post.append(f[i + 1] - even[i] + turned)
    return post


def streamed(field, direction, block, half, row):
    step_x, step_y, step_z = SPEEDS[direction]
    lane = lax.broadcasted_iota(jnp.int32, (8, LANES), 1)

    def source(from_block):
        own = field[SLOT[direction], from_block, half, pl.ds(row - step_x, 8), :]
        if step_y == 0:
            return own
        other = field[SLOT[direction], from_block, 1 - half, pl.ds(row - step_x, 8), :]
        edge = lane >= LANES - B if step_y == 1 else lane < B
        return jnp.where(edge, other, own)

    inner = rolled(source(block), B * step_y + step_z)
    if step_z == 0:
        return inner
    beside = lax.rem(block + 3 - step_z, 3)
    outer = rolled(source(beside), B * step_y - (B - 1) * step_z)
    return jnp.where(lane % B == (0 if step_z == 1 else B - 1), outer, inner)


def kernel(
    populations, solidity, home_count, evolved,
    held, held_solid, *rest,
):
    pieces = CHUNKS * AVG
    sent, arrived = rest[:pieces], rest[pieces : 2 * pieces]
    (
        first, second, up_out, down_out, up_in, down_in, result,
        load_sem, move_send, move_recv, halo_send, halo_recv,
    ) = rest[2 * pieces :]
    n_grp, n_dev = lax.axis_size("grp"), lax.axis_size("dev")
    grp, dev = lax.axis_index("grp"), lax.axis_index("dev")
    before_g, after_g = lax.rem(grp + n_grp - 1, n_grp), lax.rem(grp + 1, n_grp)
    before_d, after_d = lax.rem(dev + n_dev - 1, n_dev), lax.rem(dev + 1, n_dev)
    member = lax.rem(dev, TEAM)
    team = lax.div(dev, TEAM)

    loads = [pltpu.make_async_copy(populations, held, load_sem.at[HS])] + [
        pltpu.make_async_copy(solidity.at[pl.ds(slot, 1)], held_solid.at[slot], load_sem.at[slot]) for slot in range(HS)
    ]
    for load in loads:
        load.start()
    around = [
        (grp, before_d), (grp, after_d), (before_g, dev), (after_g, dev),
        (before_g, before_d), (before_g, after_d), (after_g, before_d), (after_g, after_d),
    ]
    barrier = pltpu.get_barrier_semaphore()
    for device in around:
        pl.semaphore_signal(barrier, inc=1, device_id=device, device_id_type=MESH)

    counts = [home_count[0, team, j] for j in range(TEAM)]
    ends = []
    for j in range(TEAM):
        ends.append(counts[j] + (ends[-1] if ends else 0))
    start = jnp.int32(0)
    for j in range(1, TEAM):
        start = jnp.where(member == j, ends[j - 1], start)

    def local_slot(block):
        return jnp.clip(block - start, 0, HS - 1)

    def origin(block):
        holder = jnp.int32(0)
        for j in range(TEAM):
            holder = holder + (ends[j] <= block).astype(jnp.int32)
        return jnp.clip(holder - member + 1, 0, 2)

    for load in loads:
        load.wait()

    def stage(target, place, block, chunk):
        slot = local_slot(block)
        for k in range(PER_CHUNK):
            lanes = pl.ds((chunk * PER_CHUNK + k) * LANES, LANES)
            target[place, pl.ds(k * Q, 8), :] = held[slot, 0:8, lanes]
            target[place, pl.ds(k * Q + 8, 8), :] = held[slot, 8:16, lanes]
            target[place, pl.ds(k * Q + 16, 3), :] = held[slot, 16:19, lanes]
            target[place, pl.ds(CELL_ROWS + k, 1), :] = held_solid[slot, :, lanes]

    def to_before(piece):
        return pltpu.make_async_remote_copy(
            src_ref=sent[piece].at[0], dst_ref=arrived[piece].at[2], send_sem=move_send.at[0, piece],
            recv_sem=move_recv.at[0, piece], device_id=(grp, before_d), device_id_type=MESH,
        )

    def to_after(piece):
        return pltpu.make_async_remote_copy(
            src_ref=sent[piece].at[1], dst_ref=arrived[piece].at[0], send_sem=move_send.at[1, piece],
            recv_sem=move_recv.at[1, piece], device_id=(grp, after_d), device_id_type=MESH,
        )

    for piece in range(pieces):
        chunk, block = piece // AVG, piece % AVG
        stage(sent[piece], 0, AVG * (member - 1) + block, chunk)
        stage(sent[piece], 1, AVG * (member + 1) + block, chunk)
        if piece == 0:
            pl.semaphore_wait(barrier, len(around))

        @pl.when(member > 0)
        def _():
            to_before(piece).start()

        @pl.when(member < TEAM - 1)
        def _():
            to_after(piece).start()

    for piece in range(pieces):
        stage(arrived[piece], 1, AVG * member + piece % AVG, piece // AVG)

    for piece in range(pieces):
        chunk, block = piece // AVG, piece % AVG

        @pl.when(member > 0)
        def _():
            to_after(piece).wait_recv()

        @pl.when(member < TEAM - 1)
        def _():
            to_before(piece).wait_recv()

        where_from = origin(AVG * member + block)
        box = arrived[piece]
        for half in range(2):
            f = [box[where_from, pl.ds(half * Q + d, 8, stride=2 * Q), :] for d in range(Q)]
            n = box[where_from, pl.ds(CELL_ROWS + half, 8, stride=2), :]
            rows = pl.ds(MAIN + 8 * chunk, 8)
            for d, value in enumerate(collide(f, n) + [n]):
                first[SLOT[d], block, half, rows, :] = value

    def packed(face, block, half, row):
        lane = lax.broadcasted_iota(jnp.int32, (8, LANES), 1) % B
        out = []
        for items in face:
            total = None
            for place, (d, z) in enumerate(items):
                value = rolled(first[SLOT[d], block, half, pl.ds(row, 8), :], place - z)
                total = value if total is None else jnp.where(lane == place, value, total)
            out.append(total)
        return out

    def halo(index, source, target, device):
        return pltpu.make_async_remote_copy(
            src_ref=source, dst_ref=target, send_sem=halo_send.at[index], recv_sem=halo_recv.at[index],
            device_id=device, device_id_type=MESH,
        )

    low, high, body = pl.ds(MAIN - 2, 2), pl.ds(MAIN + B, 2), pl.ds(MAIN, B)
    top, bottom = pl.ds(MAIN + B - 2, 2), pl.ds(MAIN, 2)
    end, begin = pl.ds(B - 2, 2), pl.ds(0, 2)
    to_g, to_b = pl.ds(0, FORWARD), pl.ds(SLOTS - FORWARD, FORWARD)
    own = pl.ds(0, AVG)
    across = [
        halo(0, first.at[to_g, own, :, top, :], first.at[to_g, own, :, low, :], (after_g, dev)),
        halo(1, first.at[to_b, own, :, bottom, :], first.at[to_b, own, :, high, :], (before_g, dev)),
    ]
    along = [
        halo(2, up_out, up_in.at[:, :, body, :], (grp, after_d)),
        halo(3, up_out.at[:, :, end, :], up_in.at[:, :, low, :], (after_g, after_d)),
        halo(4, up_out.at[:, :, begin, :], up_in.at[:, :, high, :], (before_g, after_d)),
        halo(5, down_out, down_in.at[:, :, body, :], (grp, before_d)),
        halo(6, down_out.at[:, :, end, :], down_in.at[:, :, low, :], (after_g, before_d)),
        halo(7, down_out.at[:, :, begin, :], down_in.at[:, :, high, :], (before_g, before_d)),
    ]
    for copy in across:
        copy.start()
    for half in range(2):
        for part in range(2):
            for face, block, out in ((UP_FACE, AVG - 1, up_out), (DOWN_FACE, 0, down_out)):
                for place, value in enumerate(packed(face, block, half, MAIN + 8 * part)):
                    out[place, half, pl.ds(8 * part, 8), :] = value
    for copy in along:
        copy.start()
    for copy in across + along:
        copy.wait()

    lane = lax.broadcasted_iota(jnp.int32, (8, LANES), 1) % B
    faces = ((UP_FACE, up_in), (DOWN_FACE, down_in))

    @pl.loop(0, 8)
    def _(unit):
        half = lax.rem(unit, 2)
        rows = pl.ds(pl.multiple_of(lax.div(unit, 2) * 8, 8), 8)
        came = [[box[place, half, rows, :] for place in range(2)] for _, box in faces]
        for d in range(SLOTS):
            total = None
            for (face, _), vregs in zip(faces, came):
                for items, vreg in zip(face, vregs):
                    for place, (direction, z) in enumerate(items):
                        if direction == d:
                            value = rolled(vreg, z - place)
                            total = value if total is None else jnp.where(lane == z, value, total)
            first[SLOT[d], AVG, half, rows, :] = total

    @pl.loop(0, 6)
    def _(unit):
        block, half = lax.div(unit, 2), lax.rem(unit, 2)
        for part in range(NEXT_ROWS // 8):
            row = MAIN - 1 + 8 * part
            f = [streamed(first, d, block, half, row) for d in range(Q)]
            n = first[SLOT[SOLID], block, half, pl.ds(row, 8), :]
            for d, value in enumerate(collide(f, n)):
                second[SLOT[d], block, half, pl.ds(8 * part, 8), :] = value

    @pl.loop(0, 4)
    def _(unit):
        block, half = lax.div(unit, 2), lax.rem(unit, 2)
        for part in range(B // 8):
            for d in range(Q):
                value = streamed(second, d, block, half, 1 + 8 * part)
                result[block, pl.ds((16 * part + half) * Q + d, 8, stride=2 * Q), :] = value

    @pl.loop(0, AVG)
    def _(block):
        for k in range(TILES):
            lanes = pl.ds(k * LANES, LANES)
            evolved[block, 0:8, lanes] = result[block, pl.ds(k * Q, 8), :]
            evolved[block, 8:16, lanes] = result[block, pl.ds(k * Q + 8, 8), :]
            evolved[block, 16:19, lanes] = result[block, pl.ds(k * Q + 16, 3), :]

    for piece in range(pieces):
        @pl.when(member > 0)
        def _():
            to_before(piece).wait_send()

        @pl.when(member < TEAM - 1)
        def _():
            to_after(piece).wait_send()


def on_device(populations, solidity, home_count):
    pieces = CHUNKS * AVG
    f32 = jnp.float32
    return pl.pallas_call(
        kernel,
        out_shape=jax.ShapeDtypeStruct((AVG, Q, C), f32),
        in_specs=[
            pl.BlockSpec(memory_space=pl.ANY),
            pl.BlockSpec(memory_space=pl.ANY),
            pl.BlockSpec(memory_space=pltpu.SMEM),
        ],
        out_specs=pl.BlockSpec(memory_space=pltpu.VMEM),
        scratch_shapes=[
            pltpu.VMEM((HS, Q, C), f32),
            pltpu.VMEM((HS, 1, C), f32),
            *[pltpu.VMEM((2, CHUNK_ROWS, LANES), f32) for _ in range(pieces)],
            *[pltpu.VMEM((3, CHUNK_ROWS, LANES), f32) for _ in range(pieces)],
            pltpu.VMEM((SLOTS, AVG + 1, 2, ROWS, LANES), f32),
            pltpu.VMEM((SLOTS, AVG + 1, 2, NEXT_ROWS, LANES), f32),
            pltpu.VMEM((2, 2, B, LANES), f32),
            pltpu.VMEM((2, 2, B, LANES), f32),
            pltpu.VMEM((2, 2, ROWS, LANES), f32),
            pltpu.VMEM((2, 2, ROWS, LANES), f32),
            pltpu.VMEM((AVG, TILES * Q, LANES), f32),
            pltpu.SemaphoreType.DMA((HS + 1,)),
            pltpu.SemaphoreType.DMA((2, pieces)),
            pltpu.SemaphoreType.DMA((2, pieces)),
            pltpu.SemaphoreType.DMA((8,)),
            pltpu.SemaphoreType.DMA((8,)),
        ],
        compiler_params=pltpu.CompilerParams(
            collective_id=0, has_side_effects=True, vmem_limit_bytes=48 * 1024 * 1024
        ),
        cost_estimate=pl.CostEstimate(flops=8_000_000, bytes_accessed=3_000_000, transcendentals=0),
    )(populations, solidity, home_count)


def solution(mesh):
    return jax.shard_map(
        on_device,
        mesh=mesh,
        in_specs=(P(("grp", "dev"), None, None), P(("grp", "dev"), None), P("grp", None, None)),
        out_specs=P(("grp", "dev"), None, None),
        check_vma=False,
    )
```

```python
import jax
import jax.numpy as jnp
import numpy as np
from jax import lax
from jax.experimental import pallas as pl
from jax.experimental.pallas import tpu as pltpu
from jax.sharding import PartitionSpec as P

MESH = pl.DeviceIdType.MESH
B = 16
AVG = 2
HS = 4
TEAM = 4
Q = 19
C = B * B * B
LANES = 128
TILES = C // LANES
SOLID = Q
FIELDS = Q + 1
HALVES = 2
MAIN = 8
ROWS = 32
NEXT_ROWS = 24
OUTER = [(0, 5), (11, 5)]
INNER = [(5, 6)]
CHUNKS = [OUTER, INNER]
DEPTH = [sum(size for _, size in spans) for spans in CHUNKS]

SPEEDS = [
    (0, 0, 0), (1, 0, 0), (-1, 0, 0), (0, 1, 0), (0, -1, 0), (0, 0, 1), (0, 0, -1), (1, 1, 0), (-1, -1, 0), (1, -1, 0),
    (-1, 1, 0), (1, 0, 1), (-1, 0, -1), (1, 0, -1), (-1, 0, 1), (0, 1, 1), (0, -1, -1), (0, 1, -1), (0, -1, 1),
]
ORDER = (
    [d for d in range(Q) if SPEEDS[d][0] == 1]
    + [SOLID]
    + [d for d in range(Q) if SPEEDS[d][0] == 0]
    + [d for d in range(Q) if SPEEDS[d][0] == -1]
)
SLOT = {d: place for place, d in enumerate(ORDER)}
FORWARD = 15

UP_FACE = [
    [(d, 15) for d in range(Q) if SPEEDS[d][2] >= 0] + [(SOLID, 15)],
    [(d, 14) for d in range(Q) if SPEEDS[d][2] == 1],
]
DOWN_FACE = [
    [(d, 0) for d in range(Q) if SPEEDS[d][2] <= 0] + [(SOLID, 0)],
    [(d, 1) for d in range(Q) if SPEEDS[d][2] == -1],
]


def rolled(value, amount):
    amount %= LANES
    return pltpu.roll(value, amount, 1) if amount else value


def collide(f, n):
    pair = {}
    gap = {}
    for i in range(1, Q, 2):
        pair[i] = f[i] + f[i + 1]
        gap[i] = f[i] - f[i + 1]
    xy, xz, yz = pair[7] + pair[9], pair[11] + pair[13], pair[15] + pair[17]
    axes_yz = pair[3] + pair[5]
    axes = pair[1] + axes_yz
    xy_xz = xy + xz
    diagonals = xy_xz + yz
    rho = f[0] + axes + diagonals
    energy = 8.0 * diagonals - 11.0 * axes - 30.0 * f[0]
    energy_2 = diagonals - 4.0 * axes + 12.0 * f[0]
    axial = 2.0 * pair[1] - axes_yz
    planar = xy_xz - 2.0 * yz
    axial_w = pair[3] - pair[5]
    planar_w = xy - xz
    gx_xy, gx_xz = gap[7] + gap[9], gap[11] + gap[13]
    gy_xy, gy_yz = gap[7] - gap[9], gap[15] + gap[17]
    gz_xz, gz_yz = gap[11] - gap[13], gap[15] - gap[17]
    dx, dy, dz = gx_xy + gx_xz, gy_xy + gy_yz, gz_xz + gz_yz
    jx, jy, jz = gap[1] + dx, gap[3] + dy, gap[5] + dz
    third = 1.0 / 3.0
    xx, yy, zz = jx * jx, jy * jy, jz * jz
    yyzz = yy + zz
    square = xx + yyzz
    p = (2.0 * third) * xx - third * yyzz
    w = third * (yy - zz)
    open_share = 1.0 - n

    def relaxed(rate, norm, excess):
        return (rate / norm) * excess

    r_e = open_share * relaxed(1.19, 2394.0, energy + 11.0 * rho - (19.0 * third) * square)
    r_e2 = open_share * relaxed(1.4, 252.0, energy_2 - 3.0 * rho + (5.5 * third) * square)
    r_p = open_share * relaxed(1.25, 36.0, axial + planar - p)
    r_p2 = open_share * relaxed(1.4, 72.0, planar - 2.0 * axial + 0.5 * p)
    r_w = open_share * relaxed(1.25, 12.0, axial_w + planar_w - w)
    r_w2 = open_share * relaxed(1.4, 24.0, planar_w - 2.0 * axial_w + 0.5 * w)
    third_j = (third * jx, third * jy)
    r_xy = open_share * relaxed(1.25, 4.0, pair[7] - pair[9] - third_j[0] * jy)
    r_yz = open_share * relaxed(1.25, 4.0, pair[15] - pair[17] - third_j[1] * jz)
    r_xz = open_share * relaxed(1.25, 4.0, pair[11] - pair[13] - third_j[0] * jz)
    r_qx = open_share * relaxed(1.2, 40.0, dx - 4.0 * gap[1] + (2.0 * third) * jx)
    r_qy = open_share * relaxed(1.2, 40.0, dy - 4.0 * gap[3] + (2.0 * third) * jy)
    r_qz = open_share * relaxed(1.2, 40.0, dz - 4.0 * gap[5] + (2.0 * third) * jz)
    r_mx = open_share * relaxed(1.98, 8.0, gx_xy - gx_xz)
    r_my = open_share * relaxed(1.98, 8.0, gy_yz - gy_xy)
    r_mz = open_share * relaxed(1.98, 8.0, gz_xz - gz_yz)

    even_axis = -11.0 * r_e - 4.0 * r_e2
    even_plane = 8.0 * r_e + r_e2
    a_p = r_p - 2.0 * r_p2
    a_w = r_w - 2.0 * r_w2
    d_p = r_p + r_p2
    d_w = r_w + r_w2
    axis_rest = even_axis - a_p
    plane_x = even_plane + d_p
    even_xy, even_xz, even_yz = plane_x + d_w, plane_x - d_w, even_plane - 2.0 * d_p
    x_plus, x_minus = r_qx + r_mx, r_qx - r_mx
    y_plus, y_minus = r_qy + r_my, r_qy - r_my
    z_plus, z_minus = r_qz + r_mz, r_qz - r_mz
    even = {
        1: even_axis + 2.0 * a_p,
        3: axis_rest + a_w,
        5: axis_rest - a_w,
        7: even_xy + r_xy,
        9: even_xy - r_xy,
        11: even_xz + r_xz,
        13: even_xz - r_xz,
        15: even_yz + r_yz,
        17: even_yz - r_yz,
    }
    odd = {
        1: -4.0 * r_qx,
        3: -4.0 * r_qy,
        5: -4.0 * r_qz,
        7: x_plus + y_minus,
        9: x_plus - y_minus,
        11: x_minus + z_plus,
        13: x_minus - z_plus,
        15: y_plus + z_minus,
        17: y_plus - z_minus,
    }
    post = [f[0] - (12.0 * r_e2 - 30.0 * r_e)]
    for i in range(1, Q, 2):
        turned = n * gap[i] + odd[i]
        post.append(f[i] - even[i] - turned)
        post.append(f[i + 1] - even[i] + turned)
    return post


def streamed(field, direction, block, half, row, size):
    step_x, step_y, step_z = SPEEDS[direction]
    lane = lax.broadcasted_iota(jnp.int32, (size, LANES), 1)

    def source(from_block):
        own = field[SLOT[direction], from_block, half, pl.ds(row - step_x, size), :]
        if step_y == 0:
            return own
        other = field[SLOT[direction], from_block, 1 - half, pl.ds(row - step_x, size), :]
        edge = lane >= LANES - B if step_y == 1 else lane < B
        return jnp.where(edge, other, own)

    inner = rolled(source(block), B * step_y + step_z)
    if step_z == 0:
        return inner
    beside = lax.rem(block + 3 - step_z, 3)
    outer = rolled(source(beside), B * step_y - (B - 1) * step_z)
    return jnp.where(lane % B == (0 if step_z == 1 else B - 1), outer, inner)


def kernel(populations, solidity, home_count, evolved, held, counted, *rest):
    pieces = [(chunk, block) for chunk in range(len(CHUNKS)) for block in range(AVG)]
    sent, arrived = rest[: len(pieces)], rest[len(pieces) : 2 * len(pieces)]
    (
        first, second, up_outer, up_inner, down_outer, down_inner, up_outer_in, up_inner_in, up_corner_in,
        down_outer_in, down_inner_in, down_corner_in, load_sem, move_send, move_recv, halo_send, halo_recv,
    ) = rest[2 * len(pieces) :]
    n_grp, n_dev = lax.axis_size("grp"), lax.axis_size("dev")
    grp, dev = lax.axis_index("grp"), lax.axis_index("dev")
    before_g, after_g = lax.rem(grp + n_grp - 1, n_grp), lax.rem(grp + 1, n_grp)
    before_d, after_d = lax.rem(dev + n_dev - 1, n_dev), lax.rem(dev + 1, n_dev)
    member = lax.rem(dev, TEAM)
    team = lax.div(dev, TEAM)

    loads = [
        pltpu.make_async_copy(home_count, counted, load_sem.at[0]),
        pltpu.make_async_copy(populations, held.at[pl.ds(0, Q * TILES * HS)], load_sem.at[1]),
        pltpu.make_async_copy(solidity, held.at[pl.ds(Q * TILES * HS, TILES * HS)], load_sem.at[2]),
    ]
    for load in loads:
        load.start()
    around = [
        (grp, before_d), (grp, after_d), (before_g, dev), (after_g, dev),
        (before_g, before_d), (before_g, after_d), (after_g, before_d), (after_g, after_d),
    ]
    barrier = pltpu.get_barrier_semaphore()
    for device in around:
        pl.semaphore_signal(barrier, inc=1, device_id=device, device_id_type=MESH)
    for load in loads:
        load.wait()

    ends = []
    for j in range(TEAM):
        ends.append(counted[0, j, team] + (ends[-1] if ends else 0))
    start = jnp.int32(0)
    for j in range(1, TEAM):
        start = jnp.where(member == j, ends[j - 1], start)

    def origin(block):
        holder = jnp.int32(0)
        for j in range(TEAM):
            holder = holder + (ends[j] <= block).astype(jnp.int32)
        return jnp.clip(holder - member + 1, 0, 2)

    def stage(target, place, block, chunk):
        slot = jnp.clip(block - start, 0, HS - 1)
        stride = HS * HALVES
        for half in range(HALVES):
            for field in range(FIELDS):
                to = field * DEPTH[chunk]
                for x, size in CHUNKS[chunk]:
                    at = (field * TILES + HALVES * x + half) * HS
                    target[place, half, pl.ds(to, size), :] = held[pl.ds(at + slot, size, stride=stride), :]
                    to += size

    def to_before(piece):
        return pltpu.make_async_remote_copy(
            src_ref=sent[piece].at[0], dst_ref=arrived[piece].at[2], send_sem=move_send.at[0, piece],
            recv_sem=move_recv.at[0, piece], device_id=(grp, before_d), device_id_type=MESH,
        )

    def to_after(piece):
        return pltpu.make_async_remote_copy(
            src_ref=sent[piece].at[1], dst_ref=arrived[piece].at[0], send_sem=move_send.at[1, piece],
            recv_sem=move_recv.at[1, piece], device_id=(grp, after_d), device_id_type=MESH,
        )

    for piece, (chunk, block) in enumerate(pieces):
        stage(sent[piece], 0, AVG * (member - 1) + block, chunk)
        stage(sent[piece], 1, AVG * (member + 1) + block, chunk)
        if piece == 0:
            pl.semaphore_wait(barrier, len(around))

        @pl.when(member > 0)
        def _():
            to_before(piece).start()

        @pl.when(member < TEAM - 1)
        def _():
            to_after(piece).start()

    for piece, (chunk, block) in enumerate(pieces):
        stage(arrived[piece], 1, AVG * member + block, chunk)

    def settle(piece):
        chunk, block = pieces[piece]

        @pl.when(member > 0)
        def _():
            to_after(piece).wait_recv()

        @pl.when(member < TEAM - 1)
        def _():
            to_before(piece).wait_recv()

        place = origin(AVG * member + block)
        box = arrived[piece]
        for half in range(HALVES):
            begin = 0
            for x, size in CHUNKS[chunk]:
                f = [box[place, half, pl.ds(d * DEPTH[chunk] + begin, size), :] for d in range(FIELDS)]
                for d, value in enumerate(collide(f[:Q], f[SOLID]) + f[Q:]):
                    first[SLOT[d], block, half, pl.ds(MAIN + x, size), :] = value
                begin += size

    def pack(face, block, spans, target):
        for half in range(HALVES):
            for part, (x, size) in enumerate(spans):
                lane = lax.broadcasted_iota(jnp.int32, (size, LANES), 1) % B
                for place, items in enumerate(face):
                    total = None
                    for slot, (d, z) in enumerate(items):
                        value = rolled(first[SLOT[d], block, half, pl.ds(MAIN + x, size), :], slot - z)
                        total = value if total is None else jnp.where(lane == slot, value, total)
                    target[place, half, pl.ds(8 * part, size), :] = total

    def unpack(up, down, spans):
        for part, (begin, x, size) in enumerate(spans):
            lane = lax.broadcasted_iota(jnp.int32, (size, LANES), 1) % B

            @pl.loop(0, HALVES)
            def _(half):
                came = [[box[place, half, pl.ds(begin, size), :] for place in range(2)] for box in (up, down)]
                for d in range(FIELDS):
                    total = None
                    for face, vregs in zip((UP_FACE, DOWN_FACE), came):
                        for items, vreg in zip(face, vregs):
                            for slot, (direction, z) in enumerate(items):
                                if direction == d:
                                    value = rolled(vreg, z - slot)
                                    total = value if total is None else jnp.where(lane == z, value, total)
                    first[SLOT[d], AVG, half, pl.ds(MAIN + x, size), :] = total

    def halo(index, source, target, device):
        return pltpu.make_async_remote_copy(
            src_ref=source, dst_ref=target, send_sem=halo_send.at[index], recv_sem=halo_recv.at[index],
            device_id=device, device_id_type=MESH,
        )

    low, high = pl.ds(MAIN - 2, 2), pl.ds(MAIN + B, 2)
    top, bottom = pl.ds(MAIN + B - 2, 2), pl.ds(MAIN, 2)
    end, begin = pl.ds(8 + OUTER[1][1] - 2, 2), pl.ds(0, 2)
    to_g, to_b = pl.ds(0, FORWARD), pl.ds(FIELDS - FORWARD, FORWARD)
    own = pl.ds(0, AVG)
    across = [
        halo(0, first.at[to_g, own, :, top, :], first.at[to_g, own, :, low, :], (after_g, dev)),
        halo(1, first.at[to_b, own, :, bottom, :], first.at[to_b, own, :, high, :], (before_g, dev)),
    ]
    outer = [
        halo(2, up_outer, up_outer_in, (grp, after_d)),
        halo(3, down_outer, down_outer_in, (grp, before_d)),
        halo(4, up_outer.at[:, :, end, :], up_corner_in.at[:, :, pl.ds(0, 2), :], (after_g, after_d)),
        halo(5, up_outer.at[:, :, begin, :], up_corner_in.at[:, :, pl.ds(2, 2), :], (before_g, after_d)),
        halo(6, down_outer.at[:, :, end, :], down_corner_in.at[:, :, pl.ds(0, 2), :], (after_g, before_d)),
        halo(7, down_outer.at[:, :, begin, :], down_corner_in.at[:, :, pl.ds(2, 2), :], (before_g, before_d)),
    ]
    inner = [
        halo(8, up_inner, up_inner_in, (grp, after_d)),
        halo(9, down_inner, down_inner_in, (grp, before_d)),
    ]

    def step(spans):
        def once(block, half, x, size, keep):
            f = [streamed(first, d, block, half, MAIN + x, size) for d in range(Q)]
            n = first[SLOT[SOLID], block, half, pl.ds(MAIN + x, size), :]
            for d, value in enumerate(collide(f, n)):
                if d in keep:
                    second[SLOT[d], block, half, pl.ds(x + 1, size), :] = value

        @pl.loop(0, AVG * HALVES)
        def _(unit):
            for x, size in spans:
                once(lax.div(unit, 2), lax.rem(unit, 2), x, size, range(Q))

        @pl.loop(0, HALVES)
        def _(half):
            for x, size in spans:
                once(AVG, half, x, size, [d for d in range(Q) if SPEEDS[d][2]])

    settle(0)
    settle(1)
    for copy in across:
        copy.start()
    pack(UP_FACE, AVG - 1, OUTER, up_outer)
    pack(DOWN_FACE, 0, OUTER, down_outer)
    for copy in outer:
        copy.start()
    settle(2)
    settle(3)
    pack(UP_FACE, AVG - 1, INNER, up_inner)
    pack(DOWN_FACE, 0, INNER, down_inner)
    for copy in inner:
        copy.start()
    for copy in across + outer:
        copy.wait()
    unpack(up_outer_in, down_outer_in, [(0, 0, 5), (8, 11, 5)])
    unpack(up_corner_in, down_corner_in, [(0, -2, 2), (2, B, 2)])
    step([(-1, 5), (12, 5)])
    for copy in inner:
        copy.wait()
    unpack(up_inner_in, down_inner_in, [(0, 5, 6)])
    step([(4, 8)])

    for block in range(AVG):
        for half in range(HALVES):
            for x in range(0, B, 8):
                for d in range(Q):
                    at = (d * TILES + HALVES * x + half) * AVG + block
                    evolved[pl.ds(at, 8, stride=AVG * HALVES), :] = streamed(second, d, block, half, x + 1, 8)

    for piece in range(len(pieces)):
        @pl.when(member > 0)
        def _():
            to_before(piece).wait_send()

        @pl.when(member < TEAM - 1)
        def _():
            to_after(piece).wait_send()


def on_device(populations, solidity, home_count):
    f32 = jnp.float32
    populations = populations.transpose(1, 0, 2).reshape(Q, HS, TILES, LANES).transpose(0, 2, 1, 3).reshape(-1, LANES)
    solidity = solidity.reshape(HS, TILES, LANES).transpose(1, 0, 2).reshape(-1, LANES)
    home_count = home_count.transpose(0, 2, 1)
    arguments = [pltpu.with_memory_space_constraint(a, pltpu.HBM) for a in (populations, solidity, home_count)]

    def boxes(places):
        return [pltpu.VMEM((places, HALVES, FIELDS * depth, LANES), f32) for depth in DEPTH for _ in range(AVG)]

    def faces():
        return [pltpu.VMEM((2, HALVES, 16, LANES), f32), pltpu.VMEM((2, HALVES, 8, LANES), f32)]

    copies = len(CHUNKS) * AVG
    evolved = pl.pallas_call(
        kernel,
        out_shape=jax.ShapeDtypeStruct((Q * TILES * AVG, LANES), f32),
        in_specs=[pl.BlockSpec(memory_space=pltpu.HBM)] * 3,
        out_specs=pl.BlockSpec(memory_space=pltpu.VMEM),
        scratch_shapes=[
            pltpu.VMEM((FIELDS * TILES * HS, LANES), f32),
            pltpu.SMEM(home_count.shape, jnp.int32),
            *boxes(2),
            *boxes(3),
            pltpu.VMEM((FIELDS, AVG + 1, HALVES, ROWS, LANES), f32),
            pltpu.VMEM((FIELDS, AVG + 1, HALVES, NEXT_ROWS, LANES), f32),
            *faces(),
            *faces(),
            *faces(),
            pltpu.VMEM((2, HALVES, 8, LANES), f32),
            *faces(),
            pltpu.VMEM((2, HALVES, 8, LANES), f32),
            pltpu.SemaphoreType.DMA((3,)),
            pltpu.SemaphoreType.DMA((2, copies)),
            pltpu.SemaphoreType.DMA((2, copies)),
            pltpu.SemaphoreType.DMA((10,)),
            pltpu.SemaphoreType.DMA((10,)),
        ],
        compiler_params=pltpu.CompilerParams(
            collective_id=0, has_side_effects=True, vmem_limit_bytes=48 * 1024 * 1024
        ),
        cost_estimate=pl.CostEstimate(flops=8_000_000, bytes_accessed=3_000_000, transcendentals=0),
    )(*arguments)
    return evolved.reshape(Q, TILES, AVG, LANES).transpose(2, 0, 1, 3).reshape(AVG, Q, C)


def solution(mesh):
    return jax.shard_map(
        on_device,
        mesh=mesh,
        in_specs=(P(("grp", "dev"), None, None), P(("grp", "dev"), None), P("grp", None, None)),
        out_specs=P(("grp", "dev"), None, None),
        check_vma=False,
    )
```

```python
import jax
import jax.numpy as jnp
import numpy as np
from jax import lax
from jax.experimental import pallas as pl
from jax.experimental.pallas import tpu as pltpu
from jax.sharding import PartitionSpec as P

MESH = pl.DeviceIdType.MESH
B = 16
AVG = 2
HS = 4
TEAM = 4
Q = 19
C = B * B * B
LANES = 128
TILES = C // LANES
SOLID = Q
FIELDS = Q + 1
HALVES = 2
MAIN = 8
ROWS = 32
NEXT_ROWS = 24
OUTER = [[(half, x, 2) for half in range(HALVES) for x in (0, 14)]]
MIDDLE = [[(half, 2, 4), (half, 10, 4)] for half in range(HALVES)]
CORE = [[(half, 6, 4) for half in range(HALVES)]]
CHUNKS = [OUTER, MIDDLE, CORE]
PARTS = B // 8

SPEEDS = [
    (0, 0, 0), (1, 0, 0), (-1, 0, 0), (0, 1, 0), (0, -1, 0), (0, 0, 1), (0, 0, -1), (1, 1, 0), (-1, -1, 0), (1, -1, 0),
    (-1, 1, 0), (1, 0, 1), (-1, 0, -1), (1, 0, -1), (-1, 0, 1), (0, 1, 1), (0, -1, -1), (0, 1, -1), (0, -1, 1),
]
ORDER = (
    [d for d in range(Q) if SPEEDS[d][0] == 1]
    + [SOLID]
    + [d for d in range(Q) if SPEEDS[d][0] == 0]
    + [d for d in range(Q) if SPEEDS[d][0] == -1]
)
SLOT = {d: place for place, d in enumerate(ORDER)}
FORWARD = 15

UP_FACE = [
    [(d, 15) for d in range(Q) if SPEEDS[d][2] >= 0] + [(SOLID, 15)],
    [(d, 14) for d in range(Q) if SPEEDS[d][2] == 1],
]
DOWN_FACE = [
    [(d, 0) for d in range(Q) if SPEEDS[d][2] <= 0] + [(SOLID, 0)],
    [(d, 1) for d in range(Q) if SPEEDS[d][2] == -1],
]


def rolled(value, amount):
    amount %= LANES
    return pltpu.roll(value, amount, 1) if amount else value


def collide(f, n):
    pair = {}
    gap = {}
    for i in range(1, Q, 2):
        pair[i] = f[i] + f[i + 1]
        gap[i] = f[i] - f[i + 1]
    xy, xz, yz = pair[7] + pair[9], pair[11] + pair[13], pair[15] + pair[17]
    axes_yz = pair[3] + pair[5]
    axes = pair[1] + axes_yz
    xy_xz = xy + xz
    diagonals = xy_xz + yz
    rho = f[0] + axes + diagonals
    energy = 8.0 * diagonals - 11.0 * axes - 30.0 * f[0]
    energy_2 = diagonals - 4.0 * axes + 12.0 * f[0]
    axial = 2.0 * pair[1] - axes_yz
    planar = xy_xz - 2.0 * yz
    axial_w = pair[3] - pair[5]
    planar_w = xy - xz
    gx_xy, gx_xz = gap[7] + gap[9], gap[11] + gap[13]
    gy_xy, gy_yz = gap[7] - gap[9], gap[15] + gap[17]
    gz_xz, gz_yz = gap[11] - gap[13], gap[15] - gap[17]
    dx, dy, dz = gx_xy + gx_xz, gy_xy + gy_yz, gz_xz + gz_yz
    jx, jy, jz = gap[1] + dx, gap[3] + dy, gap[5] + dz
    third = 1.0 / 3.0
    xx, yy, zz = jx * jx, jy * jy, jz * jz
    yyzz = yy + zz
    square = xx + yyzz
    p = (2.0 * third) * xx - third * yyzz
    w = third * (yy - zz)
    open_share = 1.0 - n

    def relaxed(rate, norm, excess):
        return (rate / norm) * excess

    r_e = open_share * relaxed(1.19, 2394.0, energy + 11.0 * rho - (19.0 * third) * square)
    r_e2 = open_share * relaxed(1.4, 252.0, energy_2 - 3.0 * rho + (5.5 * third) * square)
    r_p = open_share * relaxed(1.25, 36.0, axial + planar - p)
    r_p2 = open_share * relaxed(1.4, 72.0, planar - 2.0 * axial + 0.5 * p)
    r_w = open_share * relaxed(1.25, 12.0, axial_w + planar_w - w)
    r_w2 = open_share * relaxed(1.4, 24.0, planar_w - 2.0 * axial_w + 0.5 * w)
    third_j = (third * jx, third * jy)
    r_xy = open_share * relaxed(1.25, 4.0, pair[7] - pair[9] - third_j[0] * jy)
    r_yz = open_share * relaxed(1.25, 4.0, pair[15] - pair[17] - third_j[1] * jz)
    r_xz = open_share * relaxed(1.25, 4.0, pair[11] - pair[13] - third_j[0] * jz)
    r_qx = open_share * relaxed(1.2, 40.0, dx - 4.0 * gap[1] + (2.0 * third) * jx)
    r_qy = open_share * relaxed(1.2, 40.0, dy - 4.0 * gap[3] + (2.0 * third) * jy)
    r_qz = open_share * relaxed(1.2, 40.0, dz - 4.0 * gap[5] + (2.0 * third) * jz)
    r_mx = open_share * relaxed(1.98, 8.0, gx_xy - gx_xz)
    r_my = open_share * relaxed(1.98, 8.0, gy_yz - gy_xy)
    r_mz = open_share * relaxed(1.98, 8.0, gz_xz - gz_yz)

    even_axis = -11.0 * r_e - 4.0 * r_e2
    even_plane = 8.0 * r_e + r_e2
    a_p = r_p - 2.0 * r_p2
    a_w = r_w - 2.0 * r_w2
    d_p = r_p + r_p2
    d_w = r_w + r_w2
    axis_rest = even_axis - a_p
    plane_x = even_plane + d_p
    even_xy, even_xz, even_yz = plane_x + d_w, plane_x - d_w, even_plane - 2.0 * d_p
    x_plus, x_minus = r_qx + r_mx, r_qx - r_mx
    y_plus, y_minus = r_qy + r_my, r_qy - r_my
    z_plus, z_minus = r_qz + r_mz, r_qz - r_mz
    even = {
        1: even_axis + 2.0 * a_p,
        3: axis_rest + a_w,
        5: axis_rest - a_w,
        7: even_xy + r_xy,
        9: even_xy - r_xy,
        11: even_xz + r_xz,
        13: even_xz - r_xz,
        15: even_yz + r_yz,
        17: even_yz - r_yz,
    }
    odd = {
        1: -4.0 * r_qx,
        3: -4.0 * r_qy,
        5: -4.0 * r_qz,
        7: x_plus + y_minus,
        9: x_plus - y_minus,
        11: x_minus + z_plus,
        13: x_minus - z_plus,
        15: y_plus + z_minus,
        17: y_plus - z_minus,
    }
    post = [f[0] - (12.0 * r_e2 - 30.0 * r_e)]
    for i in range(1, Q, 2):
        turned = n * gap[i] + odd[i]
        post.append(f[i] - even[i] - turned)
        post.append(f[i + 1] - even[i] + turned)
    return post


def gathered(field, slot, block, half, runs, base):
    rows = sum(size for _, size in runs)
    line = lax.broadcasted_iota(jnp.int32, (rows, LANES), 0)
    value, done = None, 0
    for x, size in runs:
        part = field[slot, block, half, pl.ds(base + x - done, rows), :]
        value = part if value is None else jnp.where(line >= done, part, value)
        done += size
    return value


def streamed(field, direction, block, runs, base):
    step_x, step_y, step_z = SPEEDS[direction]
    rows = sum(size for _, size in runs)
    lane = lax.broadcasted_iota(jnp.int32, (rows, LANES), 1)

    def sources(from_block):
        halves = [gathered(field, SLOT[direction], from_block, half, runs, base - step_x) for half in range(HALVES)]
        if step_y == 0:
            return halves
        edge = lane >= LANES - B if step_y == 1 else lane < B
        return [jnp.where(edge, halves[1 - half], halves[half]) for half in range(HALVES)]

    inner = [rolled(value, B * step_y + step_z) for value in sources(block)]
    if step_z == 0:
        return inner
    beside = (block + 3 - step_z) % 3 if isinstance(block, int) else lax.rem(block + 3 - step_z, 3)
    outer = [rolled(value, B * step_y - (B - 1) * step_z) for value in sources(beside)]
    edge = lane % B == (0 if step_z == 1 else B - 1)
    return [jnp.where(edge, *both) for both in zip(outer, inner)]


def packed(face, values):
    lane = lax.broadcasted_iota(jnp.int32, (8, LANES), 1) % B
    out = []
    for items in face:
        total = None
        for slot, (d, z) in enumerate(items):
            value = rolled(values[d], slot - z)
            total = value if total is None else jnp.where(lane == slot, value, total)
        out.append(total)
    return out


def unpacked(up, down):
    lane = lax.broadcasted_iota(jnp.int32, (8, LANES), 1) % B
    out = []
    for d in range(FIELDS):
        total = None
        for face, vregs in ((UP_FACE, up), (DOWN_FACE, down)):
            for items, vreg in zip(face, vregs):
                for slot, (direction, z) in enumerate(items):
                    if direction == d:
                        value = rolled(vreg, z - slot)
                        total = value if total is None else jnp.where(lane == z, value, total)
        out.append(total)
    return out


def kernel(populations, solidity, home_count, evolved, held, counted, *rest):
    chunks = len(CHUNKS)
    sent, arrived = rest[:chunks], rest[chunks : 2 * chunks]
    (
        first, second, up_out, down_out, up_in, down_in,
        load_sem, move_send, move_recv, halo_send, halo_recv,
    ) = rest[2 * chunks :]
    n_grp, n_dev = lax.axis_size("grp"), lax.axis_size("dev")
    grp, dev = lax.axis_index("grp"), lax.axis_index("dev")
    before_g, after_g = lax.rem(grp + n_grp - 1, n_grp), lax.rem(grp + 1, n_grp)
    before_d, after_d = lax.rem(dev + n_dev - 1, n_dev), lax.rem(dev + 1, n_dev)
    before_2, after_2 = lax.rem(dev + n_dev - 2, n_dev), lax.rem(dev + 2, n_dev)
    member = lax.rem(dev, TEAM)
    team = lax.div(dev, TEAM)
    lower_pair = member < TEAM // 2

    loads = [
        pltpu.make_async_copy(home_count, counted, load_sem.at[0]),
        pltpu.make_async_copy(populations, held.at[pl.ds(0, Q * TILES * HS)], load_sem.at[1]),
        pltpu.make_async_copy(solidity, held.at[pl.ds(Q * TILES * HS, TILES * HS)], load_sem.at[2]),
    ]
    for load in loads:
        load.start()
    around = [
        (grp, before_d), (grp, after_d), (before_g, dev), (after_g, dev),
        (grp, jnp.where(lower_pair, after_2, before_2)),
    ]
    barrier = pltpu.get_barrier_semaphore()
    for device in around:
        pl.semaphore_signal(barrier, inc=1, device_id=device, device_id_type=MESH)
    for load in loads:
        load.wait()

    ends = []
    for j in range(TEAM):
        ends.append(counted[0, j, team] + (ends[-1] if ends else 0))
    start = jnp.int32(0)
    for j in range(1, TEAM):
        start = jnp.where(member == j, ends[j - 1], start)

    def holder(block):
        count = jnp.int32(0)
        for j in range(TEAM):
            count = count + (ends[j] <= block).astype(jnp.int32)
        return count

    def home(block):
        return jnp.clip(block - start, 0, HS - 1)

    def from_home(field, half, x, size, slot):
        at = (field * TILES + HALVES * x + half) * HS
        return held[pl.ds(at + slot, size, stride=HS * HALVES), :]

    def stage(target, place, block, index, chunk):
        slot = home(block)
        for field in range(FIELDS):
            to = field * 8 * len(CHUNKS[chunk])
            for vreg in CHUNKS[chunk]:
                for half, x, size in vreg:
                    target[place, index, pl.ds(to, size), :] = from_home(field, half, x, size, slot)
                    to += size

    def to_before(chunk):
        return pltpu.make_async_remote_copy(
            src_ref=sent[chunk].at[0], dst_ref=arrived[chunk].at[2], send_sem=move_send.at[0, chunk],
            recv_sem=move_recv.at[0, chunk], device_id=(grp, before_d), device_id_type=MESH,
        )

    def to_after(chunk):
        return pltpu.make_async_remote_copy(
            src_ref=sent[chunk].at[1], dst_ref=arrived[chunk].at[0], send_sem=move_send.at[1, chunk],
            recv_sem=move_recv.at[1, chunk], device_id=(grp, after_d), device_id_type=MESH,
        )

    def halo(index, source, target, device):
        return pltpu.make_async_remote_copy(
            src_ref=source, dst_ref=target, send_sem=halo_send.at[index], recv_sem=halo_recv.at[index],
            device_id=device, device_id_type=MESH,
        )

    def face_of(face, block, target, place):
        slot = home(block)

        @pl.loop(0, HALVES)
        def _(half):
            for part in range(PARTS):
                f = [from_home(field, half, 8 * part, 8, slot) for field in range(FIELDS)]
                for item, value in enumerate(packed(face, collide(f[:Q], f[SOLID]) + f[Q:])):
                    target[place, item, half, part, :, :] = value

    def up_near():
        return halo(0, up_out.at[0], up_in.at[1], (grp, after_d))

    def up_far():
        return halo(1, up_out.at[1], up_in.at[2], (grp, after_2))

    def down_near():
        return halo(2, down_out.at[0], down_in.at[1], (grp, before_d))

    def down_far():
        return halo(3, down_out.at[1], down_in.at[2], (grp, before_2))

    def move(chunk):
        @pl.when(member > 0)
        def _():
            to_before(chunk).start()

        @pl.when(member < TEAM - 1)
        def _():
            to_after(chunk).start()

    def stage_moves(chunk):
        for index in range(AVG):
            stage(sent[chunk], 0, AVG * (member - 1) + index, index, chunk)
            stage(sent[chunk], 1, AVG * (member + 1) + index, index, chunk)

    stage_moves(0)
    pl.semaphore_wait(barrier, len(around))
    move(0)
    face_of(UP_FACE, AVG * member + 1, up_out, 0)
    up_near().start()
    face_of(DOWN_FACE, AVG * member, down_out, 0)
    down_near().start()

    @pl.when(lower_pair)
    def _():
        face_of(UP_FACE, AVG * member + 3, up_out, 1)
        up_far().start()

    @pl.when(jnp.logical_not(lower_pair))
    def _():
        face_of(DOWN_FACE, AVG * member - 2, down_out, 1)
        down_far().start()

    for chunk in range(1, chunks):
        stage_moves(chunk)
        move(chunk)
    face_of(UP_FACE, AVG * member - 1, up_in, 0)
    face_of(DOWN_FACE, AVG * member + 2, down_in, 0)
    for chunk in range(chunks):
        for index in range(AVG):
            stage(arrived[chunk], 1, AVG * member + index, index, chunk)

    def put(field, block, runs, value):
        done = 0
        for half, x, size in runs:
            first[SLOT[field], block, half, pl.ds(MAIN + x, size), :] = value[done : done + size]
            done += size

    def settle(chunk):
        @pl.when(member > 0)
        def _():
            to_after(chunk).wait_recv()

        @pl.when(member < TEAM - 1)
        def _():
            to_before(chunk).wait_recv()

        box, vregs = arrived[chunk], CHUNKS[chunk]
        for index in range(AVG):
            place = jnp.clip(holder(AVG * member + index) - member + 1, 0, 2)
            for number, runs in enumerate(vregs):
                f = [box[place, index, pl.ds((d * len(vregs) + number) * 8, 8), :] for d in range(FIELDS)]
                post = collide(f[:Q], f[SOLID]) + f[Q:]
                for d, value in enumerate(post):
                    put(d, index, runs, value)

    low, high = pl.ds(MAIN - 2, 2), pl.ds(MAIN + B, 2)
    top, bottom = pl.ds(MAIN + B - 2, 2), pl.ds(MAIN, 2)
    to_g, to_b = pl.ds(0, FORWARD), pl.ds(FIELDS - FORWARD, FORWARD)

    def across(index, blocks):
        return [
            halo(index, first.at[to_g, blocks, :, top, :], first.at[to_g, blocks, :, low, :], (after_g, dev)),
            halo(index + 1, first.at[to_b, blocks, :, bottom, :], first.at[to_b, blocks, :, high, :], (before_g, dev)),
        ]

    def close(lower, upper):
        @pl.loop(0, HALVES)
        def _(half):
            for part in range(PARTS):
                values = unpacked(
                    [up_in[lower, item, half, part, :, :] for item in range(2)],
                    [down_in[upper, item, half, part, :, :] for item in range(2)],
                )
                for d, value in enumerate(values):
                    first[SLOT[d], AVG, half, pl.ds(MAIN + 8 * part, 8), :] = value

    def step(runs):
        def once(block, keep):
            f = [streamed(first, d, block, runs, MAIN) for d in range(Q)]
            for half in range(HALVES):
                n = gathered(first, SLOT[SOLID], block, half, runs, MAIN)
                post = collide([value[half] for value in f], n)
                for d in keep:
                    done = 0
                    for x, size in runs:
                        second[SLOT[d], block, half, pl.ds(x + 1, size), :] = post[d][done : done + size]
                        done += size

        @pl.loop(0, AVG)
        def _(block):
            once(block, range(Q))

        once(AVG, [d for d in range(Q) if SPEEDS[d][2]])

    def finish(runs):
        for block in range(AVG):
            for d in range(Q):
                for half, value in enumerate(streamed(second, d, block, runs, 1)):
                    done = 0
                    for x, size in runs:
                        at = (d * TILES + HALVES * x + half) * AVG + block
                        evolved[pl.ds(at, size, stride=AVG * HALVES), :] = value[done : done + size]
                        done += size

    settle(0)
    outer = across(4, pl.ds(0, AVG))
    for copy in outer:
        copy.start()
    up_near().wait_recv()
    down_near().wait_recv()

    @pl.when(lower_pair)
    def _():
        down_far().wait_recv()

    @pl.when(jnp.logical_not(lower_pair))
    def _():
        up_far().wait_recv()

    lower = jnp.where(member == 0, 1, jnp.clip(member - holder(AVG * member - 1), 0, 2))
    upper = jnp.where(member == TEAM - 1, 1, jnp.clip(holder(AVG * (member + 1)) - member, 0, 2))
    close(lower, upper)
    corners = across(6, pl.ds(AVG, 1))
    for copy in corners:
        copy.start()
    settle(1)
    for copy in outer + corners:
        copy.wait()
    step([(-1, 6), (11, 6)])
    finish([(0, 4), (12, 4)])
    settle(2)
    step([(5, 6)])
    finish([(4, 8)])

    up_near().wait_send()
    down_near().wait_send()

    @pl.when(lower_pair)
    def _():
        up_far().wait_send()

    @pl.when(jnp.logical_not(lower_pair))
    def _():
        down_far().wait_send()

    for chunk in range(chunks):
        @pl.when(member > 0)
        def _():
            to_before(chunk).wait_send()

        @pl.when(member < TEAM - 1)
        def _():
            to_after(chunk).wait_send()


def on_device(populations, solidity, home_count):
    f32 = jnp.float32
    populations = populations.transpose(1, 0, 2).reshape(Q, HS, TILES, LANES).transpose(0, 2, 1, 3).reshape(-1, LANES)
    solidity = solidity.reshape(HS, TILES, LANES).transpose(1, 0, 2).reshape(-1, LANES)
    home_count = home_count.transpose(0, 2, 1)
    arguments = [pltpu.with_memory_space_constraint(a, pltpu.HBM) for a in (populations, solidity, home_count)]

    def boxes(places):
        return [pltpu.VMEM((places, AVG, FIELDS * 8 * len(chunk), LANES), f32) for chunk in CHUNKS]

    def faces(places):
        return [pltpu.VMEM((places, 2, HALVES, PARTS, 8, LANES), f32)] * 2

    evolved = pl.pallas_call(
        kernel,
        out_shape=jax.ShapeDtypeStruct((Q * TILES * AVG, LANES), f32),
        in_specs=[pl.BlockSpec(memory_space=pltpu.HBM)] * 3,
        out_specs=pl.BlockSpec(memory_space=pltpu.VMEM),
        scratch_shapes=[
            pltpu.VMEM((FIELDS * TILES * HS, LANES), f32),
            pltpu.SMEM(home_count.shape, jnp.int32),
            *boxes(2),
            *boxes(3),
            pltpu.VMEM((FIELDS, AVG + 1, HALVES, ROWS, LANES), f32),
            pltpu.VMEM((FIELDS, AVG + 1, HALVES, NEXT_ROWS, LANES), f32),
            *faces(2),
            *faces(3),
            pltpu.SemaphoreType.DMA((3,)),
            pltpu.SemaphoreType.DMA((2, len(CHUNKS))),
            pltpu.SemaphoreType.DMA((2, len(CHUNKS))),
            pltpu.SemaphoreType.DMA((8,)),
            pltpu.SemaphoreType.DMA((8,)),
        ],
        compiler_params=pltpu.CompilerParams(
            collective_id=0, has_side_effects=True, vmem_limit_bytes=48 * 1024 * 1024
        ),
        cost_estimate=pl.CostEstimate(flops=8_000_000, bytes_accessed=3_000_000, transcendentals=0),
    )(*arguments)
    return evolved.reshape(Q, TILES, AVG, LANES).transpose(2, 0, 1, 3).reshape(AVG, Q, C)


def solution(mesh):
    return jax.shard_map(
        on_device,
        mesh=mesh,
        in_specs=(P(("grp", "dev"), None, None), P(("grp", "dev"), None), P("grp", None, None)),
        out_specs=P(("grp", "dev"), None, None),
        check_vma=False,
    )
```

```python
import jax
import jax.numpy as jnp
import numpy as np
from jax import lax
from jax.experimental import pallas as pl
from jax.experimental.pallas import tpu as pltpu
from jax.sharding import PartitionSpec as P

MESH = pl.DeviceIdType.MESH
B = 16
AVG = 2
HS = 4
TEAM = 4
Q = 19
C = B * B * B
LANES = 128
TILES = C // LANES
SOLID = Q
FIELDS = Q + 1
HALVES = 2
MAIN = 8
ROWS = 32
NEXT_ROWS = 24
OUTER = [[(half, x, 2) for half in range(HALVES) for x in (0, 14)]]
MIDDLE = [[(half, 2, 4), (half, 10, 4)] for half in range(HALVES)]
CORE = [[(half, 6, 4) for half in range(HALVES)]]
CHUNKS = [OUTER, MIDDLE, CORE]
PARTS = B // 8

SPEEDS = [
    (0, 0, 0), (1, 0, 0), (-1, 0, 0), (0, 1, 0), (0, -1, 0), (0, 0, 1), (0, 0, -1), (1, 1, 0), (-1, -1, 0), (1, -1, 0),
    (-1, 1, 0), (1, 0, 1), (-1, 0, -1), (1, 0, -1), (-1, 0, 1), (0, 1, 1), (0, -1, -1), (0, 1, -1), (0, -1, 1),
]
ORDER = (
    [d for d in range(Q) if SPEEDS[d][0] == 1]
    + [SOLID]
    + [d for d in range(Q) if SPEEDS[d][0] == 0]
    + [d for d in range(Q) if SPEEDS[d][0] == -1]
)
SLOT = {d: place for place, d in enumerate(ORDER)}
FORWARD = 15

UP_FACE = [
    [(d, 15) for d in range(Q) if SPEEDS[d][2] >= 0] + [(SOLID, 15)],
    [(d, 14) for d in range(Q) if SPEEDS[d][2] == 1],
]
DOWN_FACE = [
    [(d, 0) for d in range(Q) if SPEEDS[d][2] <= 0] + [(SOLID, 0)],
    [(d, 1) for d in range(Q) if SPEEDS[d][2] == -1],
]


def rolled(value, amount):
    amount %= LANES
    return pltpu.roll(value, amount, 1) if amount else value


def collide(f, n):
    pair = {}
    gap = {}
    for i in range(1, Q, 2):
        pair[i] = f[i] + f[i + 1]
        gap[i] = f[i] - f[i + 1]
    xy, xz, yz = pair[7] + pair[9], pair[11] + pair[13], pair[15] + pair[17]
    axes_yz = pair[3] + pair[5]
    axes = pair[1] + axes_yz
    xy_xz = xy + xz
    diagonals = xy_xz + yz
    rho = f[0] + axes + diagonals
    energy = 8.0 * diagonals - 11.0 * axes - 30.0 * f[0]
    energy_2 = diagonals - 4.0 * axes + 12.0 * f[0]
    axial = 2.0 * pair[1] - axes_yz
    planar = xy_xz - 2.0 * yz
    axial_w = pair[3] - pair[5]
    planar_w = xy - xz
    gx_xy, gx_xz = gap[7] + gap[9], gap[11] + gap[13]
    gy_xy, gy_yz = gap[7] - gap[9], gap[15] + gap[17]
    gz_xz, gz_yz = gap[11] - gap[13], gap[15] - gap[17]
    dx, dy, dz = gx_xy + gx_xz, gy_xy + gy_yz, gz_xz + gz_yz
    jx, jy, jz = gap[1] + dx, gap[3] + dy, gap[5] + dz
    third = 1.0 / 3.0
    xx, yy, zz = jx * jx, jy * jy, jz * jz
    yyzz = yy + zz
    square = xx + yyzz
    p = (2.0 * third) * xx - third * yyzz
    w = third * (yy - zz)
    open_share = 1.0 - n

    def relaxed(rate, norm, excess):
        return (rate / norm) * excess

    r_e = open_share * relaxed(1.19, 2394.0, energy + 11.0 * rho - (19.0 * third) * square)
    r_e2 = open_share * relaxed(1.4, 252.0, energy_2 - 3.0 * rho + (5.5 * third) * square)
    r_p = open_share * relaxed(1.25, 36.0, axial + planar - p)
    r_p2 = open_share * relaxed(1.4, 72.0, planar - 2.0 * axial + 0.5 * p)
    r_w = open_share * relaxed(1.25, 12.0, axial_w + planar_w - w)
    r_w2 = open_share * relaxed(1.4, 24.0, planar_w - 2.0 * axial_w + 0.5 * w)
    third_j = (third * jx, third * jy)
    r_xy = open_share * relaxed(1.25, 4.0, pair[7] - pair[9] - third_j[0] * jy)
    r_yz = open_share * relaxed(1.25, 4.0, pair[15] - pair[17] - third_j[1] * jz)
    r_xz = open_share * relaxed(1.25, 4.0, pair[11] - pair[13] - third_j[0] * jz)
    r_qx = open_share * relaxed(1.2, 40.0, dx - 4.0 * gap[1] + (2.0 * third) * jx)
    r_qy = open_share * relaxed(1.2, 40.0, dy - 4.0 * gap[3] + (2.0 * third) * jy)
    r_qz = open_share * relaxed(1.2, 40.0, dz - 4.0 * gap[5] + (2.0 * third) * jz)
    r_mx = open_share * relaxed(1.98, 8.0, gx_xy - gx_xz)
    r_my = open_share * relaxed(1.98, 8.0, gy_yz - gy_xy)
    r_mz = open_share * relaxed(1.98, 8.0, gz_xz - gz_yz)

    even_axis = -11.0 * r_e - 4.0 * r_e2
    even_plane = 8.0 * r_e + r_e2
    a_p = r_p - 2.0 * r_p2
    a_w = r_w - 2.0 * r_w2
    d_p = r_p + r_p2
    d_w = r_w + r_w2
    axis_rest = even_axis - a_p
    plane_x = even_plane + d_p
    even_xy, even_xz, even_yz = plane_x + d_w, plane_x - d_w, even_plane - 2.0 * d_p
    x_plus, x_minus = r_qx + r_mx, r_qx - r_mx
    y_plus, y_minus = r_qy + r_my, r_qy - r_my
    z_plus, z_minus = r_qz + r_mz, r_qz - r_mz
    even = {
        1: even_axis + 2.0 * a_p,
        3: axis_rest + a_w,
        5: axis_rest - a_w,
        7: even_xy + r_xy,
        9: even_xy - r_xy,
        11: even_xz + r_xz,
        13: even_xz - r_xz,
        15: even_yz + r_yz,
        17: even_yz - r_yz,
    }
    odd = {
        1: -4.0 * r_qx,
        3: -4.0 * r_qy,
        5: -4.0 * r_qz,
        7: x_plus + y_minus,
        9: x_plus - y_minus,
        11: x_minus + z_plus,
        13: x_minus - z_plus,
        15: y_plus + z_minus,
        17: y_plus - z_minus,
    }
    post = [f[0] - (12.0 * r_e2 - 30.0 * r_e)]
    for i in range(1, Q, 2):
        turned = n * gap[i] + odd[i]
        post.append(f[i] - even[i] - turned)
        post.append(f[i + 1] - even[i] + turned)
    return post


def gathered(field, slot, block, half, runs, base):
    rows = sum(size for _, size in runs)
    line = lax.broadcasted_iota(jnp.int32, (rows, LANES), 0)
    value, done = None, 0
    for x, size in runs:
        part = field[slot, block, half, pl.ds(base + x - done, rows), :]
        value = part if value is None else jnp.where(line >= done, part, value)
        done += size
    return value


def streamed(field, direction, block, runs, base):
    step_x, step_y, step_z = SPEEDS[direction]
    rows = sum(size for _, size in runs)
    lane = lax.broadcasted_iota(jnp.int32, (rows, LANES), 1)

    def sources(from_block):
        halves = [gathered(field, SLOT[direction], from_block, half, runs, base - step_x) for half in range(HALVES)]
        if step_y == 0:
            return halves
        edge = lane >= LANES - B if step_y == 1 else lane < B
        return [jnp.where(edge, halves[1 - half], halves[half]) for half in range(HALVES)]

    inner = [rolled(value, B * step_y + step_z) for value in sources(block)]
    if step_z == 0:
        return inner
    beside = (block + 3 - step_z) % 3 if isinstance(block, int) else lax.rem(block + 3 - step_z, 3)
    outer = [rolled(value, B * step_y - (B - 1) * step_z) for value in sources(beside)]
    edge = lane % B == (0 if step_z == 1 else B - 1)
    return [jnp.where(edge, *both) for both in zip(outer, inner)]


def packed(face, values):
    lane = lax.broadcasted_iota(jnp.int32, (8, LANES), 1) % B
    out = []
    for items in face:
        total = None
        for slot, (d, z) in enumerate(items):
            value = rolled(values[d], slot - z)
            total = value if total is None else jnp.where(lane == slot, value, total)
        out.append(total)
    return out


def unpacked(up, down):
    lane = lax.broadcasted_iota(jnp.int32, (8, LANES), 1) % B
    out = []
    for d in range(FIELDS):
        total = None
        for face, vregs in ((UP_FACE, up), (DOWN_FACE, down)):
            for items, vreg in zip(face, vregs):
                for slot, (direction, z) in enumerate(items):
                    if direction == d:
                        value = rolled(vreg, z - slot)
                        total = value if total is None else jnp.where(lane == z, value, total)
        out.append(total)
    return out


def kernel(populations, solidity, home_count, evolved, held, counted, *rest):
    chunks = len(CHUNKS)
    sent, arrived = rest[:chunks], rest[chunks : 2 * chunks]
    (
        first, second, up_out, down_out, up_in, down_in,
        load_sem, move_send, move_recv, halo_send, halo_recv, ready,
    ) = rest[2 * chunks :]
    n_grp, n_dev = lax.axis_size("grp"), lax.axis_size("dev")
    grp, dev = lax.axis_index("grp"), lax.axis_index("dev")
    before_g, after_g = lax.rem(grp + n_grp - 1, n_grp), lax.rem(grp + 1, n_grp)
    before_d, after_d = lax.rem(dev + n_dev - 1, n_dev), lax.rem(dev + 1, n_dev)
    before_2, after_2 = lax.rem(dev + n_dev - 2, n_dev), lax.rem(dev + 2, n_dev)
    member = lax.rem(dev, TEAM)
    team = lax.div(dev, TEAM)
    lower_pair = member < TEAM // 2

    loads = [
        pltpu.make_async_copy(home_count, counted, load_sem.at[0]),
        pltpu.make_async_copy(populations, held.at[pl.ds(0, Q * TILES * HS)], load_sem.at[1]),
        pltpu.make_async_copy(solidity, held.at[pl.ds(Q * TILES * HS, TILES * HS)], load_sem.at[2]),
    ]
    for load in loads:
        load.start()
    barrier = pltpu.get_barrier_semaphore()

    def signal(semaphore, device):
        pl.semaphore_signal(semaphore, inc=1, device_id=device, device_id_type=MESH)

    signal(barrier, (grp, before_d))

    @pl.when(member < TEAM - 1)
    def _():
        signal(barrier, (grp, after_d))

    @pl.when(lower_pair)
    def _():
        signal(barrier, (grp, after_2))

    @pl.when(grp < n_grp - 1)
    def _():
        signal(barrier, (after_g, dev))

    @pl.when(grp == 0)
    def _():
        signal(barrier, (before_g, dev))

    def enter():
        expected = jnp.minimum(member + 1, 3) + jnp.minimum(grp, 1) + jnp.where(grp == n_grp - 1, 1, 0)
        pl.semaphore_wait(barrier, expected)

        @pl.when(member == TEAM - 1)
        def _():
            signal(ready.at[0], (grp, after_d))

        @pl.when(jnp.logical_not(lower_pair))
        def _():
            signal(ready.at[1], (grp, before_2))

        @pl.when(grp > 0)
        def _():
            signal(ready.at[2], (before_g, dev))

        @pl.when(grp == n_grp - 1)
        def _():
            signal(ready.at[2], (after_g, dev))

    for load in loads:
        load.wait()

    ends = []
    for j in range(TEAM):
        ends.append(counted[0, j, team] + (ends[-1] if ends else 0))
    start = jnp.int32(0)
    for j in range(1, TEAM):
        start = jnp.where(member == j, ends[j - 1], start)

    def holder(block):
        count = jnp.int32(0)
        for j in range(TEAM):
            count = count + (ends[j] <= block).astype(jnp.int32)
        return count

    def home(block):
        return jnp.clip(block - start, 0, HS - 1)

    def from_home(field, half, x, size, slot):
        at = (field * TILES + HALVES * x + half) * HS
        return held[pl.ds(at + slot, size, stride=HS * HALVES), :]

    def stage(target, place, block, index, chunk):
        slot = home(block)
        for field in range(FIELDS):
            to = field * 8 * len(CHUNKS[chunk])
            for vreg in CHUNKS[chunk]:
                for half, x, size in vreg:
                    target[place, index, pl.ds(to, size), :] = from_home(field, half, x, size, slot)
                    to += size

    def to_before(chunk):
        return pltpu.make_async_remote_copy(
            src_ref=sent[chunk].at[0], dst_ref=arrived[chunk].at[2], send_sem=move_send.at[0, chunk],
            recv_sem=move_recv.at[0, chunk], device_id=(grp, before_d), device_id_type=MESH,
        )

    def to_after(chunk):
        return pltpu.make_async_remote_copy(
            src_ref=sent[chunk].at[1], dst_ref=arrived[chunk].at[0], send_sem=move_send.at[1, chunk],
            recv_sem=move_recv.at[1, chunk], device_id=(grp, after_d), device_id_type=MESH,
        )

    def halo(index, source, target, device):
        return pltpu.make_async_remote_copy(
            src_ref=source, dst_ref=target, send_sem=halo_send.at[index], recv_sem=halo_recv.at[index],
            device_id=device, device_id_type=MESH,
        )

    def face_of(face, block, target, place):
        slot = home(block)

        @pl.loop(0, HALVES)
        def _(half):
            for part in range(PARTS):
                f = [from_home(field, half, 8 * part, 8, slot) for field in range(FIELDS)]
                for item, value in enumerate(packed(face, collide(f[:Q], f[SOLID]) + f[Q:])):
                    target[place, item, half, part, :, :] = value

    def up_near():
        return halo(0, up_out.at[0], up_in.at[1], (grp, after_d))

    def up_far():
        return halo(1, up_out.at[1], up_in.at[2], (grp, after_2))

    def down_near():
        return halo(2, down_out.at[0], down_in.at[1], (grp, before_d))

    def down_far():
        return halo(3, down_out.at[1], down_in.at[2], (grp, before_2))

    def move(chunk):
        @pl.when(member > 0)
        def _():
            to_before(chunk).start()

        @pl.when(member < TEAM - 1)
        def _():
            to_after(chunk).start()

    def stage_moves(chunk):
        for index in range(AVG):
            stage(sent[chunk], 0, AVG * (member - 1) + index, index, chunk)
            stage(sent[chunk], 1, AVG * (member + 1) + index, index, chunk)

    @pl.when(member == TEAM - 1)
    def _():
        face_of(UP_FACE, AVG * member + 1, up_out, 0)
        enter()
        up_near().start()

    stage_moves(0)

    @pl.when(member < TEAM - 1)
    def _():
        enter()

    move(0)

    @pl.when(member < TEAM - 1)
    def _():
        face_of(UP_FACE, AVG * member + 1, up_out, 0)
        up_near().start()

    face_of(DOWN_FACE, AVG * member, down_out, 0)

    @pl.when(member > 0)
    def _():
        down_near().start()

    @pl.when(lower_pair)
    def _():
        face_of(UP_FACE, AVG * member + 3, up_out, 1)

    @pl.when(jnp.logical_not(lower_pair))
    def _():
        face_of(DOWN_FACE, AVG * member - 2, down_out, 1)
        down_far().start()

    stage_moves(1)

    @pl.when(lower_pair)
    def _():
        pl.semaphore_wait(ready.at[1], 1)
        up_far().start()

    move(1)
    stage_moves(2)
    move(2)
    face_of(UP_FACE, AVG * member - 1, up_in, 0)
    face_of(DOWN_FACE, AVG * member + 2, down_in, 0)
    for chunk in range(chunks):
        for index in range(AVG):
            stage(arrived[chunk], 1, AVG * member + index, index, chunk)

    @pl.when(member == 0)
    def _():
        pl.semaphore_wait(ready.at[0], 1)
        down_near().start()

    def put(field, block, runs, value):
        done = 0
        for half, x, size in runs:
            first[SLOT[field], block, half, pl.ds(MAIN + x, size), :] = value[done : done + size]
            done += size

    def settle(chunk):
        @pl.when(member > 0)
        def _():
            to_after(chunk).wait_recv()

        @pl.when(member < TEAM - 1)
        def _():
            to_before(chunk).wait_recv()

        box, vregs = arrived[chunk], CHUNKS[chunk]
        for index in range(AVG):
            place = jnp.clip(holder(AVG * member + index) - member + 1, 0, 2)
            for number, runs in enumerate(vregs):
                f = [box[place, index, pl.ds((d * len(vregs) + number) * 8, 8), :] for d in range(FIELDS)]
                post = collide(f[:Q], f[SOLID]) + f[Q:]
                for d, value in enumerate(post):
                    put(d, index, runs, value)

    low, high = pl.ds(MAIN - 2, 2), pl.ds(MAIN + B, 2)
    top, bottom = pl.ds(MAIN + B - 2, 2), pl.ds(MAIN, 2)
    to_g, to_b = pl.ds(0, FORWARD), pl.ds(FIELDS - FORWARD, FORWARD)

    def across(index, blocks):
        return [
            halo(index, first.at[to_g, blocks, :, top, :], first.at[to_g, blocks, :, low, :], (after_g, dev)),
            halo(index + 1, first.at[to_b, blocks, :, bottom, :], first.at[to_b, blocks, :, high, :], (before_g, dev)),
        ]

    def close(lower, upper):
        @pl.loop(0, HALVES)
        def _(half):
            for part in range(PARTS):
                values = unpacked(
                    [up_in[lower, item, half, part, :, :] for item in range(2)],
                    [down_in[upper, item, half, part, :, :] for item in range(2)],
                )
                for d, value in enumerate(values):
                    first[SLOT[d], AVG, half, pl.ds(MAIN + 8 * part, 8), :] = value

    def step(runs):
        def once(block, keep):
            f = [streamed(first, d, block, runs, MAIN) for d in range(Q)]
            for half in range(HALVES):
                n = gathered(first, SLOT[SOLID], block, half, runs, MAIN)
                post = collide([value[half] for value in f], n)
                for d in keep:
                    done = 0
                    for x, size in runs:
                        second[SLOT[d], block, half, pl.ds(x + 1, size), :] = post[d][done : done + size]
                        done += size

        @pl.loop(0, AVG)
        def _(block):
            once(block, range(Q))

        once(AVG, [d for d in range(Q) if SPEEDS[d][2]])

    def finish(runs):
        for block in range(AVG):
            for d in range(Q):
                for half, value in enumerate(streamed(second, d, block, runs, 1)):
                    done = 0
                    for x, size in runs:
                        at = (d * TILES + HALVES * x + half) * AVG + block
                        evolved[pl.ds(at, size, stride=AVG * HALVES), :] = value[done : done + size]
                        done += size

    settle(0)

    @pl.when(grp == 0)
    def _():
        pl.semaphore_wait(ready.at[2], 2)

    @pl.when(jnp.logical_and(grp > 0, grp < n_grp - 1))
    def _():
        pl.semaphore_wait(ready.at[2], 1)

    outer = across(4, pl.ds(0, AVG))
    for copy in outer:
        copy.start()
    up_near().wait_recv()
    down_near().wait_recv()

    @pl.when(lower_pair)
    def _():
        down_far().wait_recv()

    @pl.when(jnp.logical_not(lower_pair))
    def _():
        up_far().wait_recv()

    lower = jnp.where(member == 0, 1, jnp.clip(member - holder(AVG * member - 1), 0, 2))
    upper = jnp.where(member == TEAM - 1, 1, jnp.clip(holder(AVG * (member + 1)) - member, 0, 2))
    close(lower, upper)
    corners = across(6, pl.ds(AVG, 1))
    for copy in corners:
        copy.start()
    settle(1)
    step([(1, 4), (11, 4)])

    def edges():
        for copy in outer + corners:
            copy.wait()
        step([(-1, 2), (15, 2)])
        finish([(0, 4), (12, 4)])

    def core():
        settle(2)
        step([(5, 6)])
        finish([(4, 8)])

    inner = jnp.logical_and(member > 0, member < TEAM - 1)

    @pl.when(inner)
    def _():
        edges()
        core()

    @pl.when(jnp.logical_not(inner))
    def _():
        core()
        edges()

    up_near().wait_send()
    down_near().wait_send()

    @pl.when(lower_pair)
    def _():
        up_far().wait_send()

    @pl.when(jnp.logical_not(lower_pair))
    def _():
        down_far().wait_send()

    for chunk in range(chunks):
        @pl.when(member > 0)
        def _():
            to_before(chunk).wait_send()

        @pl.when(member < TEAM - 1)
        def _():
            to_after(chunk).wait_send()


def on_device(populations, solidity, home_count):
    f32 = jnp.float32
    populations = populations.transpose(1, 0, 2).reshape(Q, HS, TILES, LANES).transpose(0, 2, 1, 3).reshape(-1, LANES)
    solidity = solidity.reshape(HS, TILES, LANES).transpose(1, 0, 2).reshape(-1, LANES)
    home_count = home_count.transpose(0, 2, 1)
    arguments = [pltpu.with_memory_space_constraint(a, pltpu.HBM) for a in (populations, solidity, home_count)]

    def boxes(places):
        return [pltpu.VMEM((places, AVG, FIELDS * 8 * len(chunk), LANES), f32) for chunk in CHUNKS]

    def faces(places):
        return [pltpu.VMEM((places, 2, HALVES, PARTS, 8, LANES), f32)] * 2

    evolved = pl.pallas_call(
        kernel,
        out_shape=jax.ShapeDtypeStruct((Q * TILES * AVG, LANES), f32),
        in_specs=[pl.BlockSpec(memory_space=pltpu.HBM)] * 3,
        out_specs=pl.BlockSpec(memory_space=pltpu.VMEM),
        scratch_shapes=[
            pltpu.VMEM((FIELDS * TILES * HS, LANES), f32),
            pltpu.SMEM(home_count.shape, jnp.int32),
            *boxes(2),
            *boxes(3),
            pltpu.VMEM((FIELDS, AVG + 1, HALVES, ROWS, LANES), f32),
            pltpu.VMEM((FIELDS, AVG + 1, HALVES, NEXT_ROWS, LANES), f32),
            *faces(2),
            *faces(3),
            pltpu.SemaphoreType.DMA((3,)),
            pltpu.SemaphoreType.DMA((2, len(CHUNKS))),
            pltpu.SemaphoreType.DMA((2, len(CHUNKS))),
            pltpu.SemaphoreType.DMA((8,)),
            pltpu.SemaphoreType.DMA((8,)),
            pltpu.SemaphoreType.REGULAR((3,)),
        ],
        compiler_params=pltpu.CompilerParams(
            collective_id=0, has_side_effects=True, vmem_limit_bytes=48 * 1024 * 1024
        ),
        cost_estimate=pl.CostEstimate(flops=8_000_000, bytes_accessed=3_000_000, transcendentals=0),
    )(*arguments)
    return evolved.reshape(Q, TILES, AVG, LANES).transpose(2, 0, 1, 3).reshape(AVG, Q, C)


def solution(mesh):
    return jax.shard_map(
        on_device,
        mesh=mesh,
        in_specs=(P(("grp", "dev"), None, None), P(("grp", "dev"), None), P("grp", None, None)),
        out_specs=P(("grp", "dev"), None, None),
        check_vma=False,
    )
```

```python
import jax
import jax.numpy as jnp
import numpy as np
from jax import lax
from jax.experimental import pallas as pl
from jax.experimental.pallas import tpu as pltpu
from jax.sharding import PartitionSpec as P

MESH = pl.DeviceIdType.MESH
B = 16
AVG = 2
HS = 4
TEAM = 4
Q = 19
C = B * B * B
LANES = 128
TILES = C // LANES
SOLID = Q
FIELDS = Q + 1
HALVES = 2
MAIN = 8
ROWS = 32
NEXT_ROWS = 24
OUTER = [[(half, x, 2) for half in range(HALVES) for x in (0, 14)]]
MIDDLE = [[(half, 2, 4), (half, 10, 4)] for half in range(HALVES)]
CORE = [[(half, 6, 4) for half in range(HALVES)]]
CHUNKS = [OUTER, MIDDLE, CORE]
PARTS = B // 8

SPEEDS = [
    (0, 0, 0), (1, 0, 0), (-1, 0, 0), (0, 1, 0), (0, -1, 0), (0, 0, 1), (0, 0, -1), (1, 1, 0), (-1, -1, 0), (1, -1, 0),
    (-1, 1, 0), (1, 0, 1), (-1, 0, -1), (1, 0, -1), (-1, 0, 1), (0, 1, 1), (0, -1, -1), (0, 1, -1), (0, -1, 1),
]
ORDER = (
    [d for d in range(Q) if SPEEDS[d][0] == 1]
    + [SOLID]
    + [d for d in range(Q) if SPEEDS[d][0] == 0]
    + [d for d in range(Q) if SPEEDS[d][0] == -1]
)
SLOT = {d: place for place, d in enumerate(ORDER)}
FORWARD = 15

def face_items(near, far, step):
    wide = [(d, near) for d in range(Q) if SPEEDS[d][2] != -step] + [(SOLID, near)]
    thin = [(d, far) for d in range(Q) if SPEEDS[d][2] == step]
    return [[(half, *item) for item in wide] for half in range(HALVES)] + [
        [(half, *item) for half in range(HALVES) for item in thin]
    ]


UP_FACE = face_items(B - 1, B - 2, 1)
DOWN_FACE = face_items(0, 1, -1)


def rolled(value, amount):
    amount %= LANES
    return pltpu.roll(value, amount, 1) if amount else value


def collide(f, n):
    pair = {}
    gap = {}
    for i in range(1, Q, 2):
        pair[i] = f[i] + f[i + 1]
        gap[i] = f[i] - f[i + 1]
    xy, xz, yz = pair[7] + pair[9], pair[11] + pair[13], pair[15] + pair[17]
    axes_yz = pair[3] + pair[5]
    axes = pair[1] + axes_yz
    xy_xz = xy + xz
    diagonals = xy_xz + yz
    rho = f[0] + axes + diagonals
    energy = 8.0 * diagonals - 11.0 * axes - 30.0 * f[0]
    energy_2 = diagonals - 4.0 * axes + 12.0 * f[0]
    axial = 2.0 * pair[1] - axes_yz
    planar = xy_xz - 2.0 * yz
    axial_w = pair[3] - pair[5]
    planar_w = xy - xz
    gx_xy, gx_xz = gap[7] + gap[9], gap[11] + gap[13]
    gy_xy, gy_yz = gap[7] - gap[9], gap[15] + gap[17]
    gz_xz, gz_yz = gap[11] - gap[13], gap[15] - gap[17]
    dx, dy, dz = gx_xy + gx_xz, gy_xy + gy_yz, gz_xz + gz_yz
    jx, jy, jz = gap[1] + dx, gap[3] + dy, gap[5] + dz
    third = 1.0 / 3.0
    xx, yy, zz = jx * jx, jy * jy, jz * jz
    yyzz = yy + zz
    square = xx + yyzz
    p = (2.0 * third) * xx - third * yyzz
    w = third * (yy - zz)
    open_share = 1.0 - n

    def relaxed(rate, norm, excess):
        return (rate / norm) * excess

    r_e = open_share * relaxed(1.19, 2394.0, energy + 11.0 * rho - (19.0 * third) * square)
    r_e2 = open_share * relaxed(1.4, 252.0, energy_2 - 3.0 * rho + (5.5 * third) * square)
    r_p = open_share * relaxed(1.25, 36.0, axial + planar - p)
    r_p2 = open_share * relaxed(1.4, 72.0, planar - 2.0 * axial + 0.5 * p)
    r_w = open_share * relaxed(1.25, 12.0, axial_w + planar_w - w)
    r_w2 = open_share * relaxed(1.4, 24.0, planar_w - 2.0 * axial_w + 0.5 * w)
    third_j = (third * jx, third * jy)
    r_xy = open_share * relaxed(1.25, 4.0, pair[7] - pair[9] - third_j[0] * jy)
    r_yz = open_share * relaxed(1.25, 4.0, pair[15] - pair[17] - third_j[1] * jz)
    r_xz = open_share * relaxed(1.25, 4.0, pair[11] - pair[13] - third_j[0] * jz)
    r_qx = open_share * relaxed(1.2, 40.0, dx - 4.0 * gap[1] + (2.0 * third) * jx)
    r_qy = open_share * relaxed(1.2, 40.0, dy - 4.0 * gap[3] + (2.0 * third) * jy)
    r_qz = open_share * relaxed(1.2, 40.0, dz - 4.0 * gap[5] + (2.0 * third) * jz)
    r_mx = open_share * relaxed(1.98, 8.0, gx_xy - gx_xz)
    r_my = open_share * relaxed(1.98, 8.0, gy_yz - gy_xy)
    r_mz = open_share * relaxed(1.98, 8.0, gz_xz - gz_yz)

    even_axis = -11.0 * r_e - 4.0 * r_e2
    even_plane = 8.0 * r_e + r_e2
    a_p = r_p - 2.0 * r_p2
    a_w = r_w - 2.0 * r_w2
    d_p = r_p + r_p2
    d_w = r_w + r_w2
    axis_rest = even_axis - a_p
    plane_x = even_plane + d_p
    even_xy, even_xz, even_yz = plane_x + d_w, plane_x - d_w, even_plane - 2.0 * d_p
    x_plus, x_minus = r_qx + r_mx, r_qx - r_mx
    y_plus, y_minus = r_qy + r_my, r_qy - r_my
    z_plus, z_minus = r_qz + r_mz, r_qz - r_mz
    even = {
        1: even_axis + 2.0 * a_p,
        3: axis_rest + a_w,
        5: axis_rest - a_w,
        7: even_xy + r_xy,
        9: even_xy - r_xy,
        11: even_xz + r_xz,
        13: even_xz - r_xz,
        15: even_yz + r_yz,
        17: even_yz - r_yz,
    }
    odd = {
        1: -4.0 * r_qx,
        3: -4.0 * r_qy,
        5: -4.0 * r_qz,
        7: x_plus + y_minus,
        9: x_plus - y_minus,
        11: x_minus + z_plus,
        13: x_minus - z_plus,
        15: y_plus + z_minus,
        17: y_plus - z_minus,
    }
    post = [f[0] - (12.0 * r_e2 - 30.0 * r_e)]
    for i in range(1, Q, 2):
        turned = n * gap[i] + odd[i]
        post.append(f[i] - even[i] - turned)
        post.append(f[i + 1] - even[i] + turned)
    return post


def gathered(field, slot, block, half, runs, base):
    rows = sum(size for _, size in runs)
    line = lax.broadcasted_iota(jnp.int32, (rows, LANES), 0)
    value, done = None, 0
    for x, size in runs:
        part = field[slot, block, half, pl.ds(base + x - done, rows), :]
        value = part if value is None else jnp.where(line >= done, part, value)
        done += size
    return value


def streamed(field, direction, block, runs, base):
    step_x, step_y, step_z = SPEEDS[direction]
    rows = sum(size for _, size in runs)
    lane = lax.broadcasted_iota(jnp.int32, (rows, LANES), 1)

    def sources(from_block):
        halves = [gathered(field, SLOT[direction], from_block, half, runs, base - step_x) for half in range(HALVES)]
        if step_y == 0:
            return halves
        edge = lane >= LANES - B if step_y == 1 else lane < B
        return [jnp.where(edge, halves[1 - half], halves[half]) for half in range(HALVES)]

    inner = [rolled(value, B * step_y + step_z) for value in sources(block)]
    if step_z == 0:
        return inner
    beside = (block + 3 - step_z) % 3 if isinstance(block, int) else lax.rem(block + 3 - step_z, 3)
    outer = [rolled(value, B * step_y - (B - 1) * step_z) for value in sources(beside)]
    edge = lane % B == (0 if step_z == 1 else B - 1)
    return [jnp.where(edge, *both) for both in zip(outer, inner)]


def packed(face, values):
    lane = lax.broadcasted_iota(jnp.int32, (8, LANES), 1) % B
    out = []
    for items in face:
        total = None
        for place, (half, d, z) in enumerate(items):
            value = rolled(values[half][d], place - z)
            total = value if total is None else jnp.where(lane == place, value, total)
        out.append(total)
    return out


def unpacked(faces, half, d):
    lane = lax.broadcasted_iota(jnp.int32, (8, LANES), 1) % B
    total = None
    for face, vregs in faces:
        for items, vreg in zip(face, vregs):
            for place, (of, direction, z) in enumerate(items):
                if (of, direction) == (half, d):
                    value = rolled(vreg, z - place)
                    total = value if total is None else jnp.where(lane == z, value, total)
    return total


def kernel(populations, solidity, home_count, evolved, held, counted, *rest):
    chunks = len(CHUNKS)
    sent, arrived = rest[:chunks], rest[chunks : 2 * chunks]
    (
        first, second, up_out, down_out, relay_out, up_in, down_in, relay_up, relay_down, seam,
        load_sem, move_send, move_recv, halo_send, halo_recv, ready,
    ) = rest[2 * chunks :]
    n_grp, n_dev = lax.axis_size("grp"), lax.axis_size("dev")
    grp, dev = lax.axis_index("grp"), lax.axis_index("dev")
    before_g, after_g = lax.rem(grp + n_grp - 1, n_grp), lax.rem(grp + 1, n_grp)
    before_d, after_d = lax.rem(dev + n_dev - 1, n_dev), lax.rem(dev + 1, n_dev)
    member = lax.rem(dev, TEAM)
    team = lax.div(dev, TEAM)
    inner = jnp.logical_and(member > 0, member < TEAM - 1)
    first_dev, last_dev = dev == 0, dev == n_dev - 1

    loads = [
        pltpu.make_async_copy(home_count, counted, load_sem.at[0]),
        pltpu.make_async_copy(populations, held.at[pl.ds(0, Q * TILES * HS)], load_sem.at[1]),
        pltpu.make_async_copy(solidity, held.at[pl.ds(Q * TILES * HS, TILES * HS)], load_sem.at[2]),
    ]
    for load in loads:
        load.start()
    barrier = pltpu.get_barrier_semaphore()

    def signal(semaphore, device):
        pl.semaphore_signal(semaphore, inc=1, device_id=device, device_id_type=MESH)

    signal(barrier, (grp, before_d))

    @pl.when(member < TEAM - 1)
    def _():
        signal(barrier, (grp, after_d))

    @pl.when(grp < n_grp - 1)
    def _():
        signal(barrier, (after_g, dev))

    @pl.when(grp == 0)
    def _():
        signal(barrier, (before_g, dev))

    @pl.when(first_dev)
    def _():
        signal(barrier, (before_g, before_d))
        signal(barrier, (after_g, before_d))

    def enter():
        expected = jnp.minimum(member + 1, 2) + jnp.minimum(grp, 1) + jnp.where(grp == n_grp - 1, 1, 0)
        expected = expected + jnp.where(last_dev, 2, 0)
        pl.semaphore_wait(barrier, expected)

        @pl.when(member == TEAM - 1)
        def _():
            signal(ready.at[0], (grp, after_d))

        @pl.when(grp > 0)
        def _():
            signal(ready.at[1], (before_g, dev))

        @pl.when(grp == n_grp - 1)
        def _():
            signal(ready.at[1], (after_g, dev))

    for load in loads:
        load.wait()

    ends = []
    for j in range(TEAM):
        ends.append(counted[0, j, team] + (ends[-1] if ends else 0))
    start = jnp.int32(0)
    for j in range(1, TEAM):
        start = jnp.where(member == j, ends[j - 1], start)

    def holder(block):
        count = jnp.int32(0)
        for j in range(TEAM):
            count = count + (ends[j] <= block).astype(jnp.int32)
        return count

    def home(block):
        return jnp.clip(block - start, 0, HS - 1)

    def from_home(field, half, x, size, slot):
        at = (field * TILES + HALVES * x + half) * HS
        return held[pl.ds(at + slot, size, stride=HS * HALVES), :]

    def stage(target, place, block, index, chunk):
        slot = home(block)
        for field in range(FIELDS):
            to = field * 8 * len(CHUNKS[chunk])
            for vreg in CHUNKS[chunk]:
                for half, x, size in vreg:
                    target[place, index, pl.ds(to, size), :] = from_home(field, half, x, size, slot)
                    to += size

    def to_before(chunk):
        return pltpu.make_async_remote_copy(
            src_ref=sent[chunk].at[0], dst_ref=arrived[chunk].at[2], send_sem=move_send.at[0, chunk],
            recv_sem=move_recv.at[0, chunk], device_id=(grp, before_d), device_id_type=MESH,
        )

    def to_after(chunk):
        return pltpu.make_async_remote_copy(
            src_ref=sent[chunk].at[1], dst_ref=arrived[chunk].at[0], send_sem=move_send.at[1, chunk],
            recv_sem=move_recv.at[1, chunk], device_id=(grp, after_d), device_id_type=MESH,
        )

    def halo(index, source, target, device):
        return pltpu.make_async_remote_copy(
            src_ref=source, dst_ref=target, send_sem=halo_send.at[index], recv_sem=halo_recv.at[index],
            device_id=device, device_id_type=MESH,
        )

    def face_of(face, block, target):
        slot = home(block)

        @pl.loop(0, PARTS)
        def _(part):
            values = []
            for half in range(HALVES):
                f = [from_home(field, half, 8 * part, 8, slot) for field in range(FIELDS)]
                values.append(collide(f[:Q], f[SOLID]) + f[Q:])
            for item, value in enumerate(packed(face, values)):
                target[item, part, :, :] = value

    def up_face():
        return halo(0, up_out, up_in.at[1], (grp, after_d))

    def down_face():
        return halo(1, down_out, down_in.at[1], (grp, before_d))

    def pass_up():
        return halo(2, relay_out, relay_up, (grp, after_d))

    def pass_down():
        return halo(3, relay_out, relay_down, (grp, before_d))

    def passed(target, box, cond):
        for item in range(len(UP_FACE)):
            for part in range(PARTS):
                target[item, part, :, :] = jnp.where(cond, box[item, part, :, :], target[item, part, :, :])

    def seam_copies():
        return [
            halo(8, up_out.at[:, PARTS - 1, pl.ds(6, 2), :], seam.at[:, pl.ds(0, 2), :], (after_g, after_d)),
            halo(9, up_out.at[:, 0, pl.ds(0, 2), :], seam.at[:, pl.ds(2, 2), :], (before_g, after_d)),
        ]

    def move(chunk):
        @pl.when(member > 0)
        def _():
            to_before(chunk).start()

        @pl.when(member < TEAM - 1)
        def _():
            to_after(chunk).start()

    def stage_moves(chunk):
        for index in range(AVG):
            stage(sent[chunk], 0, AVG * (member - 1) + index, index, chunk)
            stage(sent[chunk], 1, AVG * (member + 1) + index, index, chunk)

    low, high = AVG * member, AVG * member + AVG - 1

    @pl.when(member == TEAM - 1)
    def _():
        face_of(UP_FACE, high, up_out)
        enter()
        up_face().start()

        @pl.when(last_dev)
        def _():
            for copy in seam_copies():
                copy.start()

        face_of(DOWN_FACE, low - AVG, relay_out)
        pass_down().start()
        face_of(DOWN_FACE, low, down_out)
        down_face().start()

    @pl.when(member == 0)
    def _():
        face_of(UP_FACE, high + AVG, relay_out)
        enter()
        pass_up().start()
        face_of(UP_FACE, high, up_out)
        up_face().start()

    stage_moves(0)

    @pl.when(inner)
    def _():
        enter()

    move(0)

    @pl.when(member == 1)
    def _():
        face_of(UP_FACE, high + AVG, relay_out)
        pass_up().start()
        face_of(UP_FACE, high, up_out)

    @pl.when(member == 2)
    def _():
        face_of(DOWN_FACE, low - AVG, relay_out)
        pass_down().start()
        face_of(DOWN_FACE, low, down_out)

    stage_moves(1)

    @pl.when(member == 1)
    def _():
        pass_up().wait_recv()
        passed(up_out, relay_up, holder(high) < member)
        up_face().start()

    @pl.when(member == 2)
    def _():
        pass_down().wait_recv()
        passed(down_out, relay_down, holder(low) > member)
        down_face().start()

    move(1)
    stage_moves(2)
    move(2)

    @pl.when(member < 2)
    def _():
        face_of(DOWN_FACE, low, down_out)

    @pl.when(member == 2)
    def _():
        face_of(UP_FACE, high, up_out)

    face_of(UP_FACE, low - 1, up_in.at[0])
    face_of(DOWN_FACE, high + 1, down_in.at[0])
    for chunk in range(chunks):
        for index in range(AVG):
            stage(arrived[chunk], 1, low + index, index, chunk)

    def put(field, block, runs, value):
        done = 0
        for half, x, size in runs:
            first[SLOT[field], block, half, pl.ds(MAIN + x, size), :] = value[done : done + size]
            done += size

    def settle(chunk):
        @pl.when(member > 0)
        def _():
            to_after(chunk).wait_recv()

        @pl.when(member < TEAM - 1)
        def _():
            to_before(chunk).wait_recv()

        box, vregs = arrived[chunk], CHUNKS[chunk]
        for index in range(AVG):
            place = jnp.clip(holder(AVG * member + index) - member + 1, 0, 2)
            for number, runs in enumerate(vregs):
                f = [box[place, index, pl.ds((d * len(vregs) + number) * 8, 8), :] for d in range(FIELDS)]
                post = collide(f[:Q], f[SOLID]) + f[Q:]
                for d, value in enumerate(post):
                    put(d, index, runs, value)

    below, above = pl.ds(MAIN - 2, 2), pl.ds(MAIN + B, 2)
    top, bottom = pl.ds(MAIN + B - 2, 2), pl.ds(MAIN, 2)
    to_g, to_b = pl.ds(0, FORWARD), pl.ds(FIELDS - FORWARD, FORWARD)

    def across(index, blocks):
        return [
            halo(index, first.at[to_g, blocks, :, top, :], first.at[to_g, blocks, :, below, :], (after_g, dev)),
            halo(index + 1, first.at[to_b, blocks, :, bottom, :], first.at[to_b, blocks, :, above, :], (before_g, dev)),
        ]

    def close(up, down):
        kept = lax.broadcasted_iota(jnp.int32, (8, LANES), 1) % B < B // 2
        for part in range(PARTS):
            rows = pl.ds(MAIN + 8 * part, 8)
            faces = []
            if up is not None:
                faces.append((UP_FACE, [up_in[up, item, part, :, :] for item in range(len(UP_FACE))]))
            if down is not None:
                faces.append((DOWN_FACE, [down_in[down, item, part, :, :] for item in range(len(DOWN_FACE))]))
            for half in range(HALVES):
                for d in range(FIELDS):
                    value = unpacked(faces, half, d)
                    if value is None:
                        continue
                    if down is None and not (d < Q and SPEEDS[d][2] == 1):
                        value = jnp.where(kept, first[SLOT[d], AVG, half, rows, :], value)
                    first[SLOT[d], AVG, half, rows, :] = value

    def close_seam():
        vregs = [seam[item, :, :] for item in range(len(UP_FACE))]
        kept = lax.broadcasted_iota(jnp.int32, (2, LANES), 1) % B < B // 2
        for half in range(HALVES):
            for d in range(FIELDS):
                value = unpacked([(UP_FACE, vregs)], half, d)
                if value is None:
                    continue
                for done, rows in ((0, below), (2, above)):
                    part = value[done : done + 2]
                    if not (d < Q and SPEEDS[d][2] == 1):
                        part = jnp.where(kept, first[SLOT[d], AVG, half, rows, :], part)
                    first[SLOT[d], AVG, half, rows, :] = part

    def step(runs):
        def once(block, keep):
            f = [streamed(first, d, block, runs, MAIN) for d in range(Q)]
            for half in range(HALVES):
                n = gathered(first, SLOT[SOLID], block, half, runs, MAIN)
                post = collide([value[half] for value in f], n)
                for d in keep:
                    done = 0
                    for x, size in runs:
                        second[SLOT[d], block, half, pl.ds(x + 1, size), :] = post[d][done : done + size]
                        done += size

        for block in range(AVG):
            once(block, range(Q))
        once(AVG, [d for d in range(Q) if SPEEDS[d][2]])

    def finish(runs):
        for block in range(AVG):
            for d in range(Q):
                for half, value in enumerate(streamed(second, d, block, runs, 1)):
                    done = 0
                    for x, size in runs:
                        at = (d * TILES + HALVES * x + half) * AVG + block
                        evolved[pl.ds(at, size, stride=AVG * HALVES), :] = value[done : done + size]
                        done += size

    settle(0)

    @pl.when(grp == 0)
    def _():
        pl.semaphore_wait(ready.at[1], 2)

    @pl.when(jnp.logical_and(grp > 0, grp < n_grp - 1))
    def _():
        pl.semaphore_wait(ready.at[1], 1)

    outer = across(4, pl.ds(0, AVG))
    for copy in outer:
        copy.start()
    @pl.when(member == 0)
    def _():
        pl.semaphore_wait(ready.at[0], 1)
        down_face().start()

    @pl.when(member == 1)
    def _():
        pass_down().wait_recv()
        passed(down_out, relay_down, holder(low) > member)
        down_face().start()

    @pl.when(member == 2)
    def _():
        pass_up().wait_recv()
        passed(up_out, relay_up, holder(high) < member)
        up_face().start()

    lower = jnp.where(jnp.logical_and(member > 0, holder(low - 1) == member), 0, 1)
    upper = jnp.where(jnp.logical_and(member < TEAM - 1, holder(high + 1) == member), 0, 1)
    corners = across(6, pl.ds(AVG, 1))
    down_face().wait_recv()

    @pl.when(first_dev)
    def _():
        close(None, upper)
        for copy in corners:
            copy.start()
        for copy in corners:
            copy.wait_send()
        up_face().wait_recv()
        close(lower, None)

    @pl.when(jnp.logical_not(first_dev))
    def _():
        up_face().wait_recv()
        close(lower, upper)
        for copy in corners:
            copy.start()

    settle(1)
    step([(1, 4), (11, 4)])

    def edges():
        for copy in outer:
            copy.wait()
        for copy in corners:
            copy.wait_recv()

        @pl.when(first_dev)
        def _():
            for copy in seam_copies():
                copy.wait_recv()
            close_seam()

        @pl.when(jnp.logical_not(first_dev))
        def _():
            for copy in corners:
                copy.wait_send()

        step([(-1, 2), (15, 2)])
        finish([(0, 4), (12, 4)])

    def core():
        settle(2)
        step([(5, 6)])
        finish([(4, 8)])

    @pl.when(inner)
    def _():
        edges()
        core()

    @pl.when(jnp.logical_not(inner))
    def _():
        core()
        edges()

    up_face().wait_send()
    down_face().wait_send()

    @pl.when(member < 2)
    def _():
        pass_up().wait_send()

    @pl.when(member >= 2)
    def _():
        pass_down().wait_send()

    @pl.when(last_dev)
    def _():
        for copy in seam_copies():
            copy.wait_send()

    for chunk in range(chunks):
        @pl.when(member > 0)
        def _():
            to_before(chunk).wait_send()

        @pl.when(member < TEAM - 1)
        def _():
            to_after(chunk).wait_send()


def on_device(populations, solidity, home_count):
    f32 = jnp.float32
    populations = populations.transpose(1, 0, 2).reshape(Q, HS, TILES, LANES).transpose(0, 2, 1, 3).reshape(-1, LANES)
    solidity = solidity.reshape(HS, TILES, LANES).transpose(1, 0, 2).reshape(-1, LANES)
    home_count = home_count.transpose(0, 2, 1)
    arguments = [pltpu.with_memory_space_constraint(a, pltpu.HBM) for a in (populations, solidity, home_count)]

    def boxes(places):
        return [pltpu.VMEM((places, AVG, FIELDS * 8 * len(chunk), LANES), f32) for chunk in CHUNKS]

    def faces(*places):
        return pltpu.VMEM((*places, len(UP_FACE), PARTS, 8, LANES), f32)

    evolved = pl.pallas_call(
        kernel,
        out_shape=jax.ShapeDtypeStruct((Q * TILES * AVG, LANES), f32),
        in_specs=[pl.BlockSpec(memory_space=pltpu.HBM)] * 3,
        out_specs=pl.BlockSpec(memory_space=pltpu.VMEM),
        scratch_shapes=[
            pltpu.VMEM((FIELDS * TILES * HS, LANES), f32),
            pltpu.SMEM(home_count.shape, jnp.int32),
            *boxes(2),
            *boxes(3),
            pltpu.VMEM((FIELDS, AVG + 1, HALVES, ROWS, LANES), f32),
            pltpu.VMEM((FIELDS, AVG + 1, HALVES, NEXT_ROWS, LANES), f32),
            *[faces() for _ in range(3)],
            *[faces(2) for _ in range(2)],
            *[faces() for _ in range(2)],
            pltpu.VMEM((len(UP_FACE), 8, LANES), f32),
            pltpu.SemaphoreType.DMA((3,)),
            pltpu.SemaphoreType.DMA((2, len(CHUNKS))),
            pltpu.SemaphoreType.DMA((2, len(CHUNKS))),
            pltpu.SemaphoreType.DMA((10,)),
            pltpu.SemaphoreType.DMA((10,)),
            pltpu.SemaphoreType.REGULAR((2,)),
        ],
        compiler_params=pltpu.CompilerParams(
            collective_id=0, has_side_effects=True, vmem_limit_bytes=48 * 1024 * 1024
        ),
        cost_estimate=pl.CostEstimate(flops=8_000_000, bytes_accessed=3_000_000, transcendentals=0),
    )(*arguments)
    return evolved.reshape(Q, TILES, AVG, LANES).transpose(2, 0, 1, 3).reshape(AVG, Q, C)


def solution(mesh):
    return jax.shard_map(
        on_device,
        mesh=mesh,
        in_specs=(P(("grp", "dev"), None, None), P(("grp", "dev"), None), P("grp", None, None)),
        out_specs=P(("grp", "dev"), None, None),
        check_vma=False,
    )
```

```python
import jax
import jax.numpy as jnp
import numpy as np
from jax import lax
from jax.experimental import pallas as pl
from jax.experimental.pallas import tpu as pltpu
from jax.sharding import PartitionSpec as P

MESH = pl.DeviceIdType.MESH
B = 16
AVG = 2
HS = 4
TEAM = 4
Q = 19
C = B * B * B
LANES = 128
TILES = C // LANES
SOLID = Q
FIELDS = Q + 1
HALVES = 2
MAIN = 8
ROWS = 32
NEXT_ROWS = 24
def pairs(first, last, size):
    return [(half, x, size) for x in (first, last) for half in range(HALVES)]


def halves(*runs):
    return [[(half, *run) for run in runs] for half in range(HALVES)]


CHUNKS = [[pairs(0, 14, 2)], halves((2, 3), (11, 3)), [pairs(5, 9, 2)], [[(half, 7, 2) for half in range(HALVES)]]]
PARTS = B // 8
FIELD_ROWS = TILES * HS
EDGE = 2 * HALVES * HS


def length(runs):
    return sum(size for _, _, size in runs)


DEPTH = [sum(length(runs) for runs in chunk) for chunk in CHUNKS]

SPEEDS = [
    (0, 0, 0), (1, 0, 0), (-1, 0, 0), (0, 1, 0), (0, -1, 0), (0, 0, 1), (0, 0, -1), (1, 1, 0), (-1, -1, 0), (1, -1, 0),
    (-1, 1, 0), (1, 0, 1), (-1, 0, -1), (1, 0, -1), (-1, 0, 1), (0, 1, 1), (0, -1, -1), (0, 1, -1), (0, -1, 1),
]
ORDER = (
    [d for d in range(Q) if SPEEDS[d][0] == 1]
    + [SOLID]
    + [d for d in range(Q) if SPEEDS[d][0] == 0]
    + [d for d in range(Q) if SPEEDS[d][0] == -1]
)
SLOT = {d: place for place, d in enumerate(ORDER)}
FORWARD = 15

def face_items(near, far, step):
    wide = [(d, near) for d in range(Q) if SPEEDS[d][2] != -step] + [(SOLID, near)]
    thin = [(d, far) for d in range(Q) if SPEEDS[d][2] == step]
    return [[(half, *item) for item in wide] for half in range(HALVES)] + [
        [(half, *item) for half in range(HALVES) for item in thin]
    ]


UP_FACE = face_items(B - 1, B - 2, 1)
DOWN_FACE = face_items(0, 1, -1)


def rolled(value, amount):
    amount %= LANES
    return pltpu.roll(value, amount, 1) if amount else value


def collide(f, n):
    pair = {}
    gap = {}
    for i in range(1, Q, 2):
        pair[i] = f[i] + f[i + 1]
        gap[i] = f[i] - f[i + 1]
    xy, xz, yz = pair[7] + pair[9], pair[11] + pair[13], pair[15] + pair[17]
    axes_yz = pair[3] + pair[5]
    axes = pair[1] + axes_yz
    xy_xz = xy + xz
    diagonals = xy_xz + yz
    rho = f[0] + axes + diagonals
    energy = 8.0 * diagonals - 11.0 * axes - 30.0 * f[0]
    energy_2 = diagonals - 4.0 * axes + 12.0 * f[0]
    axial = 2.0 * pair[1] - axes_yz
    planar = xy_xz - 2.0 * yz
    axial_w = pair[3] - pair[5]
    planar_w = xy - xz
    gx_xy, gx_xz = gap[7] + gap[9], gap[11] + gap[13]
    gy_xy, gy_yz = gap[7] - gap[9], gap[15] + gap[17]
    gz_xz, gz_yz = gap[11] - gap[13], gap[15] - gap[17]
    dx, dy, dz = gx_xy + gx_xz, gy_xy + gy_yz, gz_xz + gz_yz
    jx, jy, jz = gap[1] + dx, gap[3] + dy, gap[5] + dz
    third = 1.0 / 3.0
    xx, yy, zz = jx * jx, jy * jy, jz * jz
    yyzz = yy + zz
    square = xx + yyzz
    p = (2.0 * third) * xx - third * yyzz
    w = third * (yy - zz)
    open_share = 1.0 - n

    def relaxed(rate, norm, excess):
        return (rate / norm) * excess

    r_e = open_share * relaxed(1.19, 2394.0, energy + 11.0 * rho - (19.0 * third) * square)
    r_e2 = open_share * relaxed(1.4, 252.0, energy_2 - 3.0 * rho + (5.5 * third) * square)
    r_p = open_share * relaxed(1.25, 36.0, axial + planar - p)
    r_p2 = open_share * relaxed(1.4, 72.0, planar - 2.0 * axial + 0.5 * p)
    r_w = open_share * relaxed(1.25, 12.0, axial_w + planar_w - w)
    r_w2 = open_share * relaxed(1.4, 24.0, planar_w - 2.0 * axial_w + 0.5 * w)
    third_j = (third * jx, third * jy)
    r_xy = open_share * relaxed(1.25, 4.0, pair[7] - pair[9] - third_j[0] * jy)
    r_yz = open_share * relaxed(1.25, 4.0, pair[15] - pair[17] - third_j[1] * jz)
    r_xz = open_share * relaxed(1.25, 4.0, pair[11] - pair[13] - third_j[0] * jz)
    r_qx = open_share * relaxed(1.2, 40.0, dx - 4.0 * gap[1] + (2.0 * third) * jx)
    r_qy = open_share * relaxed(1.2, 40.0, dy - 4.0 * gap[3] + (2.0 * third) * jy)
    r_qz = open_share * relaxed(1.2, 40.0, dz - 4.0 * gap[5] + (2.0 * third) * jz)
    r_mx = open_share * relaxed(1.98, 8.0, gx_xy - gx_xz)
    r_my = open_share * relaxed(1.98, 8.0, gy_yz - gy_xy)
    r_mz = open_share * relaxed(1.98, 8.0, gz_xz - gz_yz)

    even_axis = -11.0 * r_e - 4.0 * r_e2
    even_plane = 8.0 * r_e + r_e2
    a_p = r_p - 2.0 * r_p2
    a_w = r_w - 2.0 * r_w2
    d_p = r_p + r_p2
    d_w = r_w + r_w2
    axis_rest = even_axis - a_p
    plane_x = even_plane + d_p
    even_xy, even_xz, even_yz = plane_x + d_w, plane_x - d_w, even_plane - 2.0 * d_p
    x_plus, x_minus = r_qx + r_mx, r_qx - r_mx
    y_plus, y_minus = r_qy + r_my, r_qy - r_my
    z_plus, z_minus = r_qz + r_mz, r_qz - r_mz
    even = {
        1: even_axis + 2.0 * a_p,
        3: axis_rest + a_w,
        5: axis_rest - a_w,
        7: even_xy + r_xy,
        9: even_xy - r_xy,
        11: even_xz + r_xz,
        13: even_xz - r_xz,
        15: even_yz + r_yz,
        17: even_yz - r_yz,
    }
    odd = {
        1: -4.0 * r_qx,
        3: -4.0 * r_qy,
        5: -4.0 * r_qz,
        7: x_plus + y_minus,
        9: x_plus - y_minus,
        11: x_minus + z_plus,
        13: x_minus - z_plus,
        15: y_plus + z_minus,
        17: y_plus - z_minus,
    }
    post = [f[0] - (12.0 * r_e2 - 30.0 * r_e)]
    for i in range(1, Q, 2):
        turned = n * gap[i] + odd[i]
        post.append(f[i] - even[i] - turned)
        post.append(f[i + 1] - even[i] + turned)
    return post


def gathered(field, slot, block, runs, base):
    rows = length(runs)
    line = lax.broadcasted_iota(jnp.int32, (rows, LANES), 0)
    value, done = None, 0
    for half, x, size in runs:
        assert 0 <= base + x - done <= field.shape[3] - rows
        part = field[slot, block, half, pl.ds(base + x - done, rows), :]
        value = part if value is None else jnp.where(line >= done, part, value)
        done += size
    return value


def streamed(field, direction, block, runs, base, known):
    step_x, step_y, step_z = SPEEDS[direction]
    lane = lax.broadcasted_iota(jnp.int32, (length(runs), LANES), 1)

    def rows_of(from_block, from_runs):
        key = (direction, from_block, tuple(from_runs))
        if key not in known:
            known[key] = gathered(field, SLOT[direction], from_block, from_runs, base - step_x)
        return known[key]

    def source(from_block):
        own = rows_of(from_block, runs)
        if step_y == 0:
            return own
        edge = lane >= LANES - B if step_y == 1 else lane < B
        return jnp.where(edge, rows_of(from_block, [(1 - half, x, size) for half, x, size in runs]), own)

    inner = rolled(source(block), B * step_y + step_z)
    if step_z == 0:
        return inner
    outer = rolled(source((block + 3 - step_z) % 3), B * step_y - (B - 1) * step_z)
    return jnp.where(lane % B == (0 if step_z == 1 else B - 1), outer, inner)


def packed(face, values):
    lane = lax.broadcasted_iota(jnp.int32, (8, LANES), 1) % B
    out = []
    for items in face:
        total = None
        for place, (half, d, z) in enumerate(items):
            value = rolled(values[half][d], place - z)
            total = value if total is None else jnp.where(lane == place, value, total)
        out.append(total)
    return out


def unpacked(faces, half, d):
    lane = lax.broadcasted_iota(jnp.int32, (8, LANES), 1) % B
    total = None
    for face, vregs in faces:
        for items, vreg in zip(face, vregs):
            for place, (of, direction, z) in enumerate(items):
                if (of, direction) == (half, d):
                    value = rolled(vreg, z - place)
                    total = value if total is None else jnp.where(lane == z, value, total)
    return total


def kernel(populations, solidity, home_count, evolved, held, outermost, counted, *rest):
    chunks = len(CHUNKS)
    sent, arrived = rest[:chunks], rest[chunks : 2 * chunks]
    (
        first, second, up_out, down_out, relay_out, up_in, down_in, relay_up, relay_down, seam,
        load_sem, move_send, move_recv, halo_send, halo_recv, ready,
    ) = rest[2 * chunks :]
    n_grp, n_dev = lax.axis_size("grp"), lax.axis_size("dev")
    grp, dev = lax.axis_index("grp"), lax.axis_index("dev")
    before_g, after_g = lax.rem(grp + n_grp - 1, n_grp), lax.rem(grp + 1, n_grp)
    before_d, after_d = lax.rem(dev + n_dev - 1, n_dev), lax.rem(dev + 1, n_dev)
    member = lax.rem(dev, TEAM)
    team = lax.div(dev, TEAM)
    inner = jnp.logical_and(member > 0, member < TEAM - 1)
    first_dev, last_dev = dev == 0, dev == n_dev - 1

    edge_rows = [(pl.ds(0, EDGE), pl.ds(0, EDGE)), (pl.ds(FIELD_ROWS - EDGE, EDGE), pl.ds(EDGE, EDGE))]
    whole = pl.ds(0, FIELD_ROWS)
    loads = [pltpu.make_async_copy(home_count, counted, load_sem.at[0])]
    for number, (rows, place, to) in enumerate([(*edge_rows[0], outermost), (*edge_rows[1], outermost), (whole, whole, held)]):
        loads.append(
            pltpu.make_async_copy(populations.at[:, rows], to.at[pl.ds(0, Q), place], load_sem.at[2 * number + 1])
        )
        loads.append(pltpu.make_async_copy(solidity.at[rows], to.at[SOLID, place], load_sem.at[2 * number + 2]))
    for load in loads:
        load.start()
    barrier = pltpu.get_barrier_semaphore()

    def signal(semaphore, device):
        pl.semaphore_signal(semaphore, inc=1, device_id=device, device_id_type=MESH)

    signal(barrier, (grp, before_d))

    @pl.when(member < TEAM - 1)
    def _():
        signal(barrier, (grp, after_d))

    @pl.when(grp < n_grp - 1)
    def _():
        signal(barrier, (after_g, dev))

    @pl.when(grp == 0)
    def _():
        signal(barrier, (before_g, dev))

    @pl.when(first_dev)
    def _():
        signal(barrier, (before_g, before_d))
        signal(barrier, (after_g, before_d))

    def enter():
        expected = jnp.minimum(member + 1, 2) + jnp.minimum(grp, 1) + jnp.where(grp == n_grp - 1, 1, 0)
        expected = expected + jnp.where(last_dev, 2, 0)
        pl.semaphore_wait(barrier, expected)

        @pl.when(member == TEAM - 1)
        def _():
            signal(ready.at[0], (grp, after_d))

        @pl.when(grp > 0)
        def _():
            signal(ready.at[1], (before_g, dev))

        @pl.when(grp == n_grp - 1)
        def _():
            signal(ready.at[1], (after_g, dev))

    for load in loads[:-2]:
        load.wait()

    ends = []
    for j in range(TEAM):
        ends.append(counted[0, j, team] + (ends[-1] if ends else 0))
    start = jnp.int32(0)
    for j in range(1, TEAM):
        start = jnp.where(member == j, ends[j - 1], start)

    def holder(block):
        count = jnp.int32(0)
        for j in range(TEAM):
            count = count + (ends[j] <= block).astype(jnp.int32)
        return count

    def home(block):
        return jnp.clip(block - start, 0, HS - 1)

    def from_home(field, half, x, size, slot):
        return held[field, pl.ds((HALVES * x + half) * HS + slot, size, stride=HS * HALVES), :]

    def stage(target, place, block, index, chunk):
        slot = home(block)
        for field in range(FIELDS):
            to = field * DEPTH[chunk]
            for vreg in CHUNKS[chunk]:
                for half, x, size in vreg:
                    if chunk == 0:
                        at = (HALVES * (x if x < 2 else x - B + 4) + half) * HS
                        value = outermost[field, pl.ds(at + slot, size, stride=HS * HALVES), :]
                    else:
                        value = from_home(field, half, x, size, slot)
                    target[place, index, pl.ds(to, size), :] = value
                    to += size

    def to_before(chunk):
        return pltpu.make_async_remote_copy(
            src_ref=sent[chunk].at[0], dst_ref=arrived[chunk].at[2], send_sem=move_send.at[0, chunk],
            recv_sem=move_recv.at[0, chunk], device_id=(grp, before_d), device_id_type=MESH,
        )

    def to_after(chunk):
        return pltpu.make_async_remote_copy(
            src_ref=sent[chunk].at[1], dst_ref=arrived[chunk].at[0], send_sem=move_send.at[1, chunk],
            recv_sem=move_recv.at[1, chunk], device_id=(grp, after_d), device_id_type=MESH,
        )

    def halo(index, source, target, device):
        return pltpu.make_async_remote_copy(
            src_ref=source, dst_ref=target, send_sem=halo_send.at[index], recv_sem=halo_recv.at[index],
            device_id=device, device_id_type=MESH,
        )

    def face_of(face, block, target):
        slot = home(block)

        @pl.loop(0, PARTS)
        def _(part):
            values = []
            for half in range(HALVES):
                f = [from_home(field, half, 8 * part, 8, slot) for field in range(FIELDS)]
                values.append(collide(f[:Q], f[SOLID]) + f[Q:])
            for item, value in enumerate(packed(face, values)):
                target[item, part, :, :] = value

    def up_face():
        return halo(0, up_out, up_in.at[1], (grp, after_d))

    def down_face():
        return halo(1, down_out, down_in.at[1], (grp, before_d))

    def pass_up():
        return halo(2, relay_out, relay_up, (grp, after_d))

    def pass_down():
        return halo(3, relay_out, relay_down, (grp, before_d))

    def passed(target, box, cond):
        for item in range(len(UP_FACE)):
            for part in range(PARTS):
                target[item, part, :, :] = jnp.where(cond, box[item, part, :, :], target[item, part, :, :])

    def seam_copies():
        return [
            halo(8, up_out.at[:, PARTS - 1, pl.ds(6, 2), :], seam.at[:, pl.ds(0, 2), :], (after_g, after_d)),
            halo(9, up_out.at[:, 0, pl.ds(0, 2), :], seam.at[:, pl.ds(2, 2), :], (before_g, after_d)),
        ]

    def move(chunk):
        @pl.when(member > 0)
        def _():
            to_before(chunk).start()

        @pl.when(member < TEAM - 1)
        def _():
            to_after(chunk).start()

    def stage_moves(chunk):
        for index in range(AVG):
            stage(sent[chunk], 0, AVG * (member - 1) + index, index, chunk)
            stage(sent[chunk], 1, AVG * (member + 1) + index, index, chunk)

    low, high = AVG * member, AVG * member + AVG - 1

    def rest_loaded():
        for load in loads[-2:]:
            load.wait()

    @pl.when(jnp.logical_not(inner))
    def _():
        rest_loaded()

    @pl.when(member == TEAM - 1)
    def _():
        face_of(UP_FACE, high, up_out)
        enter()
        up_face().start()

        @pl.when(last_dev)
        def _():
            for copy in seam_copies():
                copy.start()

        face_of(DOWN_FACE, low - AVG, relay_out)
        pass_down().start()
        face_of(DOWN_FACE, low, down_out)
        down_face().start()

    @pl.when(member == 0)
    def _():
        face_of(UP_FACE, high + AVG, relay_out)
        enter()
        pass_up().start()
        face_of(UP_FACE, high, up_out)
        up_face().start()

    stage_moves(0)

    @pl.when(inner)
    def _():
        enter()

    move(0)

    @pl.when(inner)
    def _():
        rest_loaded()

    @pl.when(member == 1)
    def _():
        face_of(UP_FACE, high + AVG, relay_out)
        pass_up().start()
        face_of(UP_FACE, high, up_out)

    @pl.when(member == 2)
    def _():
        face_of(DOWN_FACE, low - AVG, relay_out)
        pass_down().start()
        face_of(DOWN_FACE, low, down_out)

    stage_moves(1)

    @pl.when(member == 1)
    def _():
        pass_up().wait_recv()
        passed(up_out, relay_up, holder(high) < member)
        up_face().start()

    @pl.when(member == 2)
    def _():
        pass_down().wait_recv()
        passed(down_out, relay_down, holder(low) > member)
        down_face().start()

    move(1)
    for chunk in range(2, chunks):
        stage_moves(chunk)
        move(chunk)

    @pl.when(member < 2)
    def _():
        face_of(DOWN_FACE, low, down_out)

    @pl.when(member == 2)
    def _():
        face_of(UP_FACE, high, up_out)

    face_of(UP_FACE, low - 1, up_in.at[0])
    face_of(DOWN_FACE, high + 1, down_in.at[0])
    for chunk in range(chunks):
        for index in range(AVG):
            stage(arrived[chunk], 1, low + index, index, chunk)

    def put(field, block, runs, value):
        done = 0
        for half, x, size in runs:
            first[SLOT[field], block, half, pl.ds(MAIN + x, size), :] = value[done : done + size]
            done += size

    def settle(chunk):
        @pl.when(member > 0)
        def _():
            to_after(chunk).wait_recv()

        @pl.when(member < TEAM - 1)
        def _():
            to_before(chunk).wait_recv()

        box = arrived[chunk]
        for index in range(AVG):
            place = jnp.clip(holder(AVG * member + index) - member + 1, 0, 2)
            done = 0
            for runs in CHUNKS[chunk]:
                f = [box[place, index, pl.ds(d * DEPTH[chunk] + done, length(runs)), :] for d in range(FIELDS)]
                for d, value in enumerate(collide(f[:Q], f[SOLID]) + f[Q:]):
                    put(d, index, runs, value)
                done += length(runs)

    below, above = pl.ds(MAIN - 2, 2), pl.ds(MAIN + B, 2)
    top, bottom = pl.ds(MAIN + B - 2, 2), pl.ds(MAIN, 2)
    to_g, to_b = pl.ds(0, FORWARD), pl.ds(FIELDS - FORWARD, FORWARD)

    def across(index, blocks):
        return [
            halo(index, first.at[to_g, blocks, :, top, :], first.at[to_g, blocks, :, below, :], (after_g, dev)),
            halo(index + 1, first.at[to_b, blocks, :, bottom, :], first.at[to_b, blocks, :, above, :], (before_g, dev)),
        ]

    def close(up, down):
        kept = lax.broadcasted_iota(jnp.int32, (8, LANES), 1) % B < B // 2
        for part in range(PARTS):
            rows = pl.ds(MAIN + 8 * part, 8)
            faces = []
            if up is not None:
                faces.append((UP_FACE, [up_in[up, item, part, :, :] for item in range(len(UP_FACE))]))
            if down is not None:
                faces.append((DOWN_FACE, [down_in[down, item, part, :, :] for item in range(len(DOWN_FACE))]))
            for half in range(HALVES):
                for d in range(FIELDS):
                    value = unpacked(faces, half, d)
                    if value is None:
                        continue
                    if down is None and not (d < Q and SPEEDS[d][2] == 1):
                        value = jnp.where(kept, first[SLOT[d], AVG, half, rows, :], value)
                    first[SLOT[d], AVG, half, rows, :] = value

    def close_seam():
        vregs = [seam[item, :, :] for item in range(len(UP_FACE))]
        kept = lax.broadcasted_iota(jnp.int32, (2, LANES), 1) % B < B // 2
        for half in range(HALVES):
            for d in range(FIELDS):
                value = unpacked([(UP_FACE, vregs)], half, d)
                if value is None:
                    continue
                for done, rows in ((0, below), (2, above)):
                    part = value[done : done + 2]
                    if not (d < Q and SPEEDS[d][2] == 1):
                        part = jnp.where(kept, first[SLOT[d], AVG, half, rows, :], part)
                    first[SLOT[d], AVG, half, rows, :] = part

    def step(groups):
        for block in range(AVG + 1):
            known = {}
            arriving = [[streamed(first, d, block, runs, MAIN, known) for d in range(Q)] for runs in groups]
            for runs, f in zip(groups, arriving):
                post = collide(f, gathered(first, SLOT[SOLID], block, runs, MAIN))
                for d in range(Q):
                    done = 0
                    for half, x, size in runs:
                        if block < AVG or SPEEDS[d][2]:
                            second[SLOT[d], block, half, pl.ds(x + 1, size), :] = post[d][done : done + size]
                        done += size

    def finish(groups):
        for block in range(AVG):
            known = {}
            for d in range(Q):
                for runs in groups:
                    value, done = streamed(second, d, block, runs, 1, known), 0
                    for half, x, size in runs:
                        at = (d * TILES + HALVES * x + half) * AVG + block
                        evolved[pl.ds(at, size, stride=AVG * HALVES), :] = value[done : done + size]
                        done += size

    settle(0)

    @pl.when(grp == 0)
    def _():
        pl.semaphore_wait(ready.at[1], 2)

    @pl.when(jnp.logical_and(grp > 0, grp < n_grp - 1))
    def _():
        pl.semaphore_wait(ready.at[1], 1)

    outer = across(4, pl.ds(0, AVG))
    for copy in outer:
        copy.start()
    @pl.when(member == 0)
    def _():
        pl.semaphore_wait(ready.at[0], 1)
        down_face().start()

    @pl.when(member == 1)
    def _():
        pass_down().wait_recv()
        passed(down_out, relay_down, holder(low) > member)
        down_face().start()

    @pl.when(member == 2)
    def _():
        pass_up().wait_recv()
        passed(up_out, relay_up, holder(high) < member)
        up_face().start()

    lower = jnp.where(jnp.logical_and(member > 0, holder(low - 1) == member), 0, 1)
    upper = jnp.where(jnp.logical_and(member < TEAM - 1, holder(high + 1) == member), 0, 1)
    corners = across(6, pl.ds(AVG, 1))
    down_face().wait_recv()

    @pl.when(first_dev)
    def _():
        close(None, upper)
        for copy in corners:
            copy.start()
        for copy in corners:
            copy.wait_send()
        up_face().wait_recv()
        close(lower, None)

    @pl.when(jnp.logical_not(first_dev))
    def _():
        up_face().wait_recv()
        close(lower, upper)
        for copy in corners:
            copy.start()

    settle(1)
    step(halves((1, 3), (12, 3)))

    def edges():
        for copy in outer:
            copy.wait()
        for copy in corners:
            copy.wait_recv()

        @pl.when(first_dev)
        def _():
            for copy in seam_copies():
                copy.wait_recv()
            close_seam()

        @pl.when(jnp.logical_not(first_dev))
        def _():
            for copy in corners:
                copy.wait_send()

        step([pairs(-1, 15, 2)])
        finish(halves((0, 3), (13, 3)))

    def core():
        settle(2)
        step([pairs(4, 10, 2)])
        finish([pairs(3, 11, 2)])
        settle(3)
        step([[(half, 6, 4) for half in range(HALVES)]])
        finish(halves((5, 6)))

    @pl.when(inner)
    def _():
        edges()
        core()

    @pl.when(jnp.logical_not(inner))
    def _():
        core()
        edges()

    up_face().wait_send()
    down_face().wait_send()

    @pl.when(member < 2)
    def _():
        pass_up().wait_send()

    @pl.when(member >= 2)
    def _():
        pass_down().wait_send()

    @pl.when(last_dev)
    def _():
        for copy in seam_copies():
            copy.wait_send()

    for chunk in range(chunks):
        @pl.when(member > 0)
        def _():
            to_before(chunk).wait_send()

        @pl.when(member < TEAM - 1)
        def _():
            to_after(chunk).wait_send()


def on_device(populations, solidity, home_count):
    f32 = jnp.float32
    populations = populations.transpose(1, 0, 2).reshape(Q, HS, TILES, LANES).transpose(0, 2, 1, 3)
    populations = populations.reshape(Q, FIELD_ROWS, LANES)
    solidity = solidity.reshape(HS, TILES, LANES).transpose(1, 0, 2).reshape(-1, LANES)
    home_count = home_count.transpose(0, 2, 1)
    arguments = [pltpu.with_memory_space_constraint(a, pltpu.HBM) for a in (populations, solidity, home_count)]

    def boxes(places):
        return [pltpu.VMEM((places, AVG, FIELDS * depth, LANES), f32) for depth in DEPTH]

    def faces(*places):
        return pltpu.VMEM((*places, len(UP_FACE), PARTS, 8, LANES), f32)

    evolved = pl.pallas_call(
        kernel,
        out_shape=jax.ShapeDtypeStruct((Q * TILES * AVG, LANES), f32),
        in_specs=[pl.BlockSpec(memory_space=pltpu.HBM)] * 3,
        out_specs=pl.BlockSpec(memory_space=pltpu.VMEM),
        scratch_shapes=[
            pltpu.VMEM((FIELDS, FIELD_ROWS, LANES), f32),
            pltpu.VMEM((FIELDS, 2 * EDGE, LANES), f32),
            pltpu.SMEM(home_count.shape, jnp.int32),
            *boxes(2),
            *boxes(3),
            pltpu.VMEM((FIELDS, AVG + 1, HALVES, ROWS, LANES), f32),
            pltpu.VMEM((FIELDS, AVG + 1, HALVES, NEXT_ROWS, LANES), f32),
            *[faces() for _ in range(3)],
            *[faces(2) for _ in range(2)],
            *[faces() for _ in range(2)],
            pltpu.VMEM((len(UP_FACE), 8, LANES), f32),
            pltpu.SemaphoreType.DMA((7,)),
            pltpu.SemaphoreType.DMA((2, len(CHUNKS))),
            pltpu.SemaphoreType.DMA((2, len(CHUNKS))),
            pltpu.SemaphoreType.DMA((10,)),
            pltpu.SemaphoreType.DMA((10,)),
            pltpu.SemaphoreType.REGULAR((2,)),
        ],
        compiler_params=pltpu.CompilerParams(
            collective_id=0, has_side_effects=True, vmem_limit_bytes=48 * 1024 * 1024
        ),
        cost_estimate=pl.CostEstimate(flops=8_000_000, bytes_accessed=3_000_000, transcendentals=0),
    )(*arguments)
    return evolved.reshape(Q, TILES, AVG, LANES).transpose(2, 0, 1, 3).reshape(AVG, Q, C)


def solution(mesh):
    return jax.shard_map(
        on_device,
        mesh=mesh,
        in_specs=(P(("grp", "dev"), None, None), P(("grp", "dev"), None), P("grp", None, None)),
        out_specs=P(("grp", "dev"), None, None),
        check_vma=False,
    )
```

```python
import jax
import jax.numpy as jnp
import numpy as np
from jax import lax
from jax.experimental import pallas as pl
from jax.experimental.pallas import tpu as pltpu
from jax.sharding import PartitionSpec as P

MESH = pl.DeviceIdType.MESH
B = 16
AVG = 2
HS = 4
TEAM = 4
Q = 19
C = B * B * B
LANES = 128
TILES = C // LANES
SOLID = Q
FIELDS = Q + 1
HALVES = 2
MAIN = 8
ROWS = 32
def pairs(first, last, size):
    return [(half, x, size) for x in (first, last) for half in range(HALVES)]


def halves(*runs):
    return [[(half, *run) for run in runs] for half in range(HALVES)]


CHUNKS = [[pairs(0, 14, 2)], halves((2, 3), (11, 3)), [pairs(5, 9, 2)], [[(half, 7, 2) for half in range(HALVES)]]]
PARTS = B // 8
FIELD_ROWS = TILES * HS
EDGE = 2 * HALVES * HS


def length(runs):
    return sum(size for _, _, size in runs)


DEPTH = [sum(length(runs) for runs in chunk) for chunk in CHUNKS]

SPEEDS = [
    (0, 0, 0), (1, 0, 0), (-1, 0, 0), (0, 1, 0), (0, -1, 0), (0, 0, 1), (0, 0, -1), (1, 1, 0), (-1, -1, 0), (1, -1, 0),
    (-1, 1, 0), (1, 0, 1), (-1, 0, -1), (1, 0, -1), (-1, 0, 1), (0, 1, 1), (0, -1, -1), (0, 1, -1), (0, -1, 1),
]
ORDER = (
    [d for d in range(Q) if SPEEDS[d][0] == 1]
    + [SOLID]
    + [d for d in range(Q) if SPEEDS[d][0] == 0]
    + [d for d in range(Q) if SPEEDS[d][0] == -1]
)
SLOT = {d: place for place, d in enumerate(ORDER)}
FORWARD = 15

def face_items(near, far, step):
    wide = [(d, near) for d in range(Q) if SPEEDS[d][2] != -step] + [(SOLID, near)]
    thin = [(d, far) for d in range(Q) if SPEEDS[d][2] == step]
    return [[(half, *item) for item in wide] for half in range(HALVES)] + [
        [(half, *item) for half in range(HALVES) for item in thin]
    ]


UP_FACE = face_items(B - 1, B - 2, 1)
DOWN_FACE = face_items(0, 1, -1)


def rolled(value, amount):
    amount %= LANES
    return pltpu.roll(value, amount, 1) if amount else value


def collide(f, n):
    pair = {}
    gap = {}
    for i in range(1, Q, 2):
        pair[i] = f[i] + f[i + 1]
        gap[i] = f[i] - f[i + 1]
    xy, xz, yz = pair[7] + pair[9], pair[11] + pair[13], pair[15] + pair[17]
    axes_yz = pair[3] + pair[5]
    axes = pair[1] + axes_yz
    xy_xz = xy + xz
    diagonals = xy_xz + yz
    rho = f[0] + axes + diagonals
    energy = 8.0 * diagonals - 11.0 * axes - 30.0 * f[0]
    energy_2 = diagonals - 4.0 * axes + 12.0 * f[0]
    axial = 2.0 * pair[1] - axes_yz
    planar = xy_xz - 2.0 * yz
    axial_w = pair[3] - pair[5]
    planar_w = xy - xz
    gx_xy, gx_xz = gap[7] + gap[9], gap[11] + gap[13]
    gy_xy, gy_yz = gap[7] - gap[9], gap[15] + gap[17]
    gz_xz, gz_yz = gap[11] - gap[13], gap[15] - gap[17]
    dx, dy, dz = gx_xy + gx_xz, gy_xy + gy_yz, gz_xz + gz_yz
    jx, jy, jz = gap[1] + dx, gap[3] + dy, gap[5] + dz
    third = 1.0 / 3.0
    xx, yy, zz = jx * jx, jy * jy, jz * jz
    yyzz = yy + zz
    square = xx + yyzz
    p = (2.0 * third) * xx - third * yyzz
    w = third * (yy - zz)
    open_share = 1.0 - n

    def relaxed(rate, norm, excess):
        return (rate / norm) * excess

    r_e = open_share * relaxed(1.19, 2394.0, energy + 11.0 * rho - (19.0 * third) * square)
    r_e2 = open_share * relaxed(1.4, 252.0, energy_2 - 3.0 * rho + (5.5 * third) * square)
    r_p = open_share * relaxed(1.25, 36.0, axial + planar - p)
    r_p2 = open_share * relaxed(1.4, 72.0, planar - 2.0 * axial + 0.5 * p)
    r_w = open_share * relaxed(1.25, 12.0, axial_w + planar_w - w)
    r_w2 = open_share * relaxed(1.4, 24.0, planar_w - 2.0 * axial_w + 0.5 * w)
    third_j = (third * jx, third * jy)
    r_xy = open_share * relaxed(1.25, 4.0, pair[7] - pair[9] - third_j[0] * jy)
    r_yz = open_share * relaxed(1.25, 4.0, pair[15] - pair[17] - third_j[1] * jz)
    r_xz = open_share * relaxed(1.25, 4.0, pair[11] - pair[13] - third_j[0] * jz)
    r_qx = open_share * relaxed(1.2, 40.0, dx - 4.0 * gap[1] + (2.0 * third) * jx)
    r_qy = open_share * relaxed(1.2, 40.0, dy - 4.0 * gap[3] + (2.0 * third) * jy)
    r_qz = open_share * relaxed(1.2, 40.0, dz - 4.0 * gap[5] + (2.0 * third) * jz)
    r_mx = open_share * relaxed(1.98, 8.0, gx_xy - gx_xz)
    r_my = open_share * relaxed(1.98, 8.0, gy_yz - gy_xy)
    r_mz = open_share * relaxed(1.98, 8.0, gz_xz - gz_yz)

    even_axis = -11.0 * r_e - 4.0 * r_e2
    even_plane = 8.0 * r_e + r_e2
    a_p = r_p - 2.0 * r_p2
    a_w = r_w - 2.0 * r_w2
    d_p = r_p + r_p2
    d_w = r_w + r_w2
    axis_rest = even_axis - a_p
    plane_x = even_plane + d_p
    even_xy, even_xz, even_yz = plane_x + d_w, plane_x - d_w, even_plane - 2.0 * d_p
    x_plus, x_minus = r_qx + r_mx, r_qx - r_mx
    y_plus, y_minus = r_qy + r_my, r_qy - r_my
    z_plus, z_minus = r_qz + r_mz, r_qz - r_mz
    even = {
        1: even_axis + 2.0 * a_p,
        3: axis_rest + a_w,
        5: axis_rest - a_w,
        7: even_xy + r_xy,
        9: even_xy - r_xy,
        11: even_xz + r_xz,
        13: even_xz - r_xz,
        15: even_yz + r_yz,
        17: even_yz - r_yz,
    }
    odd = {
        1: -4.0 * r_qx,
        3: -4.0 * r_qy,
        5: -4.0 * r_qz,
        7: x_plus + y_minus,
        9: x_plus - y_minus,
        11: x_minus + z_plus,
        13: x_minus - z_plus,
        15: y_plus + z_minus,
        17: y_plus - z_minus,
    }
    post = [f[0] - (12.0 * r_e2 - 30.0 * r_e)]
    for i in range(1, Q, 2):
        turned = n * gap[i] + odd[i]
        post.append(f[i] - even[i] - turned)
        post.append(f[i + 1] - even[i] + turned)
    return post


def gathered(field, slot, block, runs, base):
    rows = length(runs)
    line = lax.broadcasted_iota(jnp.int32, (rows, LANES), 0)
    value, done = None, 0
    for half, x, size in runs:
        assert 0 <= base + x - done <= field.shape[3] - rows
        part = field[slot, block, half, pl.ds(base + x - done, rows), :]
        value = part if value is None else jnp.where(line >= done, part, value)
        done += size
    return value


def streamed(field, direction, block, runs, base, known):
    step_x, step_y, step_z = SPEEDS[direction]
    lane = lax.broadcasted_iota(jnp.int32, (length(runs), LANES), 1)

    def rows_of(from_block, from_runs):
        key = (direction, from_block, tuple(from_runs))
        if key not in known:
            known[key] = gathered(field, SLOT[direction], from_block, from_runs, base - step_x)
        return known[key]

    def source(from_block):
        own = rows_of(from_block, runs)
        if step_y == 0:
            return own
        edge = lane >= LANES - B if step_y == 1 else lane < B
        return jnp.where(edge, rows_of(from_block, [(1 - half, x, size) for half, x, size in runs]), own)

    inner = rolled(source(block), B * step_y + step_z)
    if step_z == 0:
        return inner
    outer = rolled(source((block + 3 - step_z) % 3), B * step_y - (B - 1) * step_z)
    return jnp.where(lane % B == (0 if step_z == 1 else B - 1), outer, inner)


def packed(face, values):
    lane = lax.broadcasted_iota(jnp.int32, (8, LANES), 1) % B
    out = []
    for items in face:
        total = None
        for place, (half, d, z) in enumerate(items):
            value = rolled(values[half][d], place - z)
            total = value if total is None else jnp.where(lane == place, value, total)
        out.append(total)
    return out


def unpacked(faces, half, d):
    lane = lax.broadcasted_iota(jnp.int32, (8, LANES), 1) % B
    total = None
    for face, vregs in faces:
        for items, vreg in zip(face, vregs):
            for place, (of, direction, z) in enumerate(items):
                if (of, direction) == (half, d):
                    value = rolled(vreg, z - place)
                    total = value if total is None else jnp.where(lane == z, value, total)
    return total


def kernel(populations, solidity, home_count, evolved, held, outermost, counted, *rest):
    chunks = len(CHUNKS)
    sent, arrived = rest[:chunks], rest[chunks : 2 * chunks]
    (
        first, second, up_out, down_out, relay_out, up_in, down_in, relay_up, relay_down, seam,
        load_sem, move_send, move_recv, halo_send, halo_recv, ready,
    ) = rest[2 * chunks :]
    n_grp, n_dev = lax.axis_size("grp"), lax.axis_size("dev")
    grp, dev = lax.axis_index("grp"), lax.axis_index("dev")
    before_g, after_g = lax.rem(grp + n_grp - 1, n_grp), lax.rem(grp + 1, n_grp)
    before_d, after_d = lax.rem(dev + n_dev - 1, n_dev), lax.rem(dev + 1, n_dev)
    member = lax.rem(dev, TEAM)
    team = lax.div(dev, TEAM)
    inner = jnp.logical_and(member > 0, member < TEAM - 1)
    first_dev, last_dev = dev == 0, dev == n_dev - 1

    edge_rows = [(pl.ds(0, EDGE), pl.ds(0, EDGE)), (pl.ds(FIELD_ROWS - EDGE, EDGE), pl.ds(EDGE, EDGE))]
    whole = pl.ds(0, FIELD_ROWS)
    loads = [pltpu.make_async_copy(home_count, counted, load_sem.at[0])]
    for number, (rows, place, to) in enumerate([(*edge_rows[0], outermost), (*edge_rows[1], outermost), (whole, whole, held)]):
        loads.append(
            pltpu.make_async_copy(populations.at[:, rows], to.at[pl.ds(0, Q), place], load_sem.at[2 * number + 1])
        )
        loads.append(pltpu.make_async_copy(solidity.at[rows], to.at[SOLID, place], load_sem.at[2 * number + 2]))
    for load in loads:
        load.start()
    barrier = pltpu.get_barrier_semaphore()

    def signal(semaphore, device):
        pl.semaphore_signal(semaphore, inc=1, device_id=device, device_id_type=MESH)

    signal(barrier, (grp, before_d))

    @pl.when(member < TEAM - 1)
    def _():
        signal(barrier, (grp, after_d))

    @pl.when(grp < n_grp - 1)
    def _():
        signal(barrier, (after_g, dev))

    @pl.when(grp == 0)
    def _():
        signal(barrier, (before_g, dev))

    @pl.when(first_dev)
    def _():
        signal(barrier, (before_g, before_d))
        signal(barrier, (after_g, before_d))

    def enter():
        expected = jnp.minimum(member + 1, 2) + jnp.minimum(grp, 1) + jnp.where(grp == n_grp - 1, 1, 0)
        expected = expected + jnp.where(last_dev, 2, 0)
        pl.semaphore_wait(barrier, expected)

    def answer():
        @pl.when(member == TEAM - 1)
        def _():
            signal(ready.at[0], (grp, after_d))

        @pl.when(grp > 0)
        def _():
            signal(ready.at[1], (before_g, dev))

        @pl.when(grp == n_grp - 1)
        def _():
            signal(ready.at[1], (after_g, dev))

    for load in loads[:-2]:
        load.wait()

    ends = []
    for j in range(TEAM):
        ends.append(counted[0, j, team] + (ends[-1] if ends else 0))
    start = jnp.int32(0)
    for j in range(1, TEAM):
        start = jnp.where(member == j, ends[j - 1], start)

    def holder(block):
        count = jnp.int32(0)
        for j in range(TEAM):
            count = count + (ends[j] <= block).astype(jnp.int32)
        return count

    def home(block):
        return jnp.clip(block - start, 0, HS - 1)

    def from_home(field, half, x, size, slot):
        return held[field, pl.ds((HALVES * x + half) * HS + slot, size, stride=HS * HALVES), :]

    def stage(target, place, block, index, chunk):
        slot = home(block)
        for field in range(FIELDS):
            to = field * DEPTH[chunk]
            for vreg in CHUNKS[chunk]:
                for half, x, size in vreg:
                    if chunk == 0:
                        at = (HALVES * (x if x < 2 else x - B + 4) + half) * HS
                        value = outermost[field, pl.ds(at + slot, size, stride=HS * HALVES), :]
                    else:
                        value = from_home(field, half, x, size, slot)
                    target[place, index, pl.ds(to, size), :] = value
                    to += size

    def to_before(chunk):
        return pltpu.make_async_remote_copy(
            src_ref=sent[chunk].at[0], dst_ref=arrived[chunk].at[2], send_sem=move_send.at[0, chunk],
            recv_sem=move_recv.at[0, chunk], device_id=(grp, before_d), device_id_type=MESH,
        )

    def to_after(chunk):
        return pltpu.make_async_remote_copy(
            src_ref=sent[chunk].at[1], dst_ref=arrived[chunk].at[0], send_sem=move_send.at[1, chunk],
            recv_sem=move_recv.at[1, chunk], device_id=(grp, after_d), device_id_type=MESH,
        )

    def halo(index, source, target, device):
        return pltpu.make_async_remote_copy(
            src_ref=source, dst_ref=target, send_sem=halo_send.at[index], recv_sem=halo_recv.at[index],
            device_id=device, device_id_type=MESH,
        )

    def face_of(face, block, target):
        slot = home(block)

        @pl.loop(0, PARTS)
        def _(part):
            values = []
            for half in range(HALVES):
                f = [from_home(field, half, 8 * part, 8, slot) for field in range(FIELDS)]
                values.append(collide(f[:Q], f[SOLID]) + f[Q:])
            for item, value in enumerate(packed(face, values)):
                target[item, part, :, :] = value

    def up_face():
        return halo(0, up_out, up_in.at[1], (grp, after_d))

    def down_face():
        return halo(1, down_out, down_in.at[1], (grp, before_d))

    def pass_up():
        return halo(2, relay_out, relay_up, (grp, after_d))

    def pass_down():
        return halo(3, relay_out, relay_down, (grp, before_d))

    def passed(target, box, cond):
        for item in range(len(UP_FACE)):
            for part in range(PARTS):
                target[item, part, :, :] = jnp.where(cond, box[item, part, :, :], target[item, part, :, :])

    def seam_copies():
        return [
            halo(8, up_out.at[:, PARTS - 1, pl.ds(6, 2), :], seam.at[:, pl.ds(0, 2), :], (after_g, after_d)),
            halo(9, up_out.at[:, 0, pl.ds(0, 2), :], seam.at[:, pl.ds(2, 2), :], (before_g, after_d)),
        ]

    def move(chunk):
        @pl.when(member > 0)
        def _():
            to_before(chunk).start()

        @pl.when(member < TEAM - 1)
        def _():
            to_after(chunk).start()

    def stage_move(chunk, place):
        for index in range(AVG):
            stage(sent[chunk], place, AVG * (member - 1 + 2 * place) + index, index, chunk)

    def stage_moves(chunk):
        stage_move(chunk, 0)
        stage_move(chunk, 1)

    low, high = AVG * member, AVG * member + AVG - 1

    def rest_loaded():
        for load in loads[-2:]:
            load.wait()

    @pl.when(jnp.logical_not(inner))
    def _():
        rest_loaded()

    @pl.when(member == TEAM - 1)
    def _():
        face_of(UP_FACE, high, up_out)
        enter()
        up_face().start()

        @pl.when(last_dev)
        def _():
            for copy in seam_copies():
                copy.start()

        answer()
        face_of(DOWN_FACE, low - AVG, relay_out)
        pass_down().start()
        face_of(DOWN_FACE, low, down_out)
        down_face().start()

    @pl.when(member == 0)
    def _():
        face_of(UP_FACE, high + AVG, relay_out)
        enter()
        pass_up().start()
        answer()
        face_of(UP_FACE, high, up_out)
        up_face().start()

    @pl.when(member == 1)
    def _():
        stage_move(0, 1)
        enter()
        to_after(0).start()
        stage_move(0, 0)
        to_before(0).start()

    @pl.when(member == 2)
    def _():
        stage_move(0, 0)
        enter()
        to_before(0).start()
        stage_move(0, 1)
        to_after(0).start()

    @pl.when(jnp.logical_not(inner))
    def _():
        stage_moves(0)
        move(0)

    @pl.when(inner)
    def _():
        answer()
        rest_loaded()

    @pl.when(member == 1)
    def _():
        face_of(UP_FACE, high + AVG, relay_out)
        pass_up().start()
        face_of(UP_FACE, high, up_out)

    @pl.when(member == 2)
    def _():
        face_of(DOWN_FACE, low - AVG, relay_out)
        pass_down().start()
        face_of(DOWN_FACE, low, down_out)

    stage_moves(1)

    @pl.when(member == 1)
    def _():
        pass_up().wait_recv()
        passed(up_out, relay_up, holder(high) < member)
        up_face().start()

    @pl.when(member == 2)
    def _():
        pass_down().wait_recv()
        passed(down_out, relay_down, holder(low) > member)
        down_face().start()

    move(1)
    for chunk in range(2, chunks):
        stage_moves(chunk)
        move(chunk)

    @pl.when(member < 2)
    def _():
        face_of(DOWN_FACE, low, down_out)

    @pl.when(member == 2)
    def _():
        face_of(UP_FACE, high, up_out)

    face_of(UP_FACE, low - 1, up_in.at[0])
    face_of(DOWN_FACE, high + 1, down_in.at[0])
    for chunk in range(chunks):
        for index in range(AVG):
            stage(arrived[chunk], 1, low + index, index, chunk)

    def put(field, block, runs, value):
        done = 0
        for half, x, size in runs:
            first[SLOT[field], block, half, pl.ds(MAIN + x, size), :] = value[done : done + size]
            done += size

    def settle(chunk):
        @pl.when(member > 0)
        def _():
            to_after(chunk).wait_recv()

        @pl.when(member < TEAM - 1)
        def _():
            to_before(chunk).wait_recv()

        box = arrived[chunk]
        for index in range(AVG):
            place = jnp.clip(holder(AVG * member + index) - member + 1, 0, 2)
            done = 0
            for runs in CHUNKS[chunk]:
                f = [box[place, index, pl.ds(d * DEPTH[chunk] + done, length(runs)), :] for d in range(FIELDS)]
                for d, value in enumerate(collide(f[:Q], f[SOLID]) + f[Q:]):
                    put(d, index, runs, value)
                done += length(runs)

    below, above = pl.ds(MAIN - 2, 2), pl.ds(MAIN + B, 2)
    top, bottom = pl.ds(MAIN + B - 2, 2), pl.ds(MAIN, 2)
    to_g, to_b = pl.ds(0, FORWARD), pl.ds(FIELDS - FORWARD, FORWARD)

    def across(index, blocks):
        return [
            halo(index, first.at[to_g, blocks, :, top, :], first.at[to_g, blocks, :, below, :], (after_g, dev)),
            halo(index + 1, first.at[to_b, blocks, :, bottom, :], first.at[to_b, blocks, :, above, :], (before_g, dev)),
        ]

    def close(up, down):
        kept = lax.broadcasted_iota(jnp.int32, (8, LANES), 1) % B < B // 2
        for part in range(PARTS):
            rows = pl.ds(MAIN + 8 * part, 8)
            faces = []
            if up is not None:
                faces.append((UP_FACE, [up_in[up, item, part, :, :] for item in range(len(UP_FACE))]))
            if down is not None:
                faces.append((DOWN_FACE, [down_in[down, item, part, :, :] for item in range(len(DOWN_FACE))]))
            for half in range(HALVES):
                for d in range(FIELDS):
                    value = unpacked(faces, half, d)
                    if value is None:
                        continue
                    if down is None and not (d < Q and SPEEDS[d][2] == 1):
                        value = jnp.where(kept, first[SLOT[d], AVG, half, rows, :], value)
                    first[SLOT[d], AVG, half, rows, :] = value

    def close_seam():
        vregs = [seam[item, :, :] for item in range(len(UP_FACE))]
        kept = lax.broadcasted_iota(jnp.int32, (2, LANES), 1) % B < B // 2
        for half in range(HALVES):
            for d in range(FIELDS):
                value = unpacked([(UP_FACE, vregs)], half, d)
                if value is None:
                    continue
                for done, rows in ((0, below), (2, above)):
                    part = value[done : done + 2]
                    if not (d < Q and SPEEDS[d][2] == 1):
                        part = jnp.where(kept, first[SLOT[d], AVG, half, rows, :], part)
                    first[SLOT[d], AVG, half, rows, :] = part

    def step(groups):
        for block in range(AVG + 1):
            known = {}
            arriving = [[streamed(first, d, block, runs, MAIN, known) for d in range(Q)] for runs in groups]
            for runs, f in zip(groups, arriving):
                post = collide(f, gathered(first, SLOT[SOLID], block, runs, MAIN))
                for d in range(Q):
                    done = 0
                    for half, x, size in runs:
                        if block < AVG or SPEEDS[d][2]:
                            second[SLOT[d], block, half, pl.ds(MAIN + x, size), :] = post[d][done : done + size]
                        done += size

    def finish(groups):
        for block in range(AVG):
            known = {}
            for d in range(Q):
                for runs in groups:
                    value, done = streamed(second, d, block, runs, MAIN, known), 0
                    for half, x, size in runs:
                        at = (d * TILES + HALVES * x + half) * AVG + block
                        evolved[pl.ds(at, size, stride=AVG * HALVES), :] = value[done : done + size]
                        done += size

    settle(0)

    @pl.when(grp == 0)
    def _():
        pl.semaphore_wait(ready.at[1], 2)

    @pl.when(jnp.logical_and(grp > 0, grp < n_grp - 1))
    def _():
        pl.semaphore_wait(ready.at[1], 1)

    outer = across(4, pl.ds(0, AVG))
    for copy in outer:
        copy.start()
    @pl.when(member == 0)
    def _():
        pl.semaphore_wait(ready.at[0], 1)
        down_face().start()

    @pl.when(member == 1)
    def _():
        pass_down().wait_recv()
        passed(down_out, relay_down, holder(low) > member)
        down_face().start()

    @pl.when(member == 2)
    def _():
        pass_up().wait_recv()
        passed(up_out, relay_up, holder(high) < member)
        up_face().start()

    lower = jnp.where(jnp.logical_and(member > 0, holder(low - 1) == member), 0, 1)
    upper = jnp.where(jnp.logical_and(member < TEAM - 1, holder(high + 1) == member), 0, 1)
    corners = across(6, pl.ds(AVG, 1))
    down_face().wait_recv()

    @pl.when(first_dev)
    def _():
        close(None, upper)
        for copy in corners:
            copy.start()
        for copy in corners:
            copy.wait_send()
        up_face().wait_recv()
        close(lower, None)

    @pl.when(jnp.logical_not(first_dev))
    def _():
        up_face().wait_recv()
        close(lower, upper)
        for copy in corners:
            copy.start()

    settle(1)
    step(halves((1, 3), (12, 3)))

    def edges():
        for copy in outer:
            copy.wait()
        for copy in corners:
            copy.wait_recv()

        @pl.when(first_dev)
        def _():
            for copy in seam_copies():
                copy.wait_recv()
            close_seam()

        @pl.when(jnp.logical_not(first_dev))
        def _():
            for copy in corners:
                copy.wait_send()

        step([pairs(-1, 15, 2)])
        finish([pairs(0, 14, 2)])

    def core():
        settle(2)
        step([pairs(4, 10, 2)])
        finish(halves((2, 3), (11, 3)))
        settle(3)
        step([[(half, 6, 4) for half in range(HALVES)]])
        finish(halves((5, 6)))

    @pl.when(inner)
    def _():
        edges()
        core()

    @pl.when(jnp.logical_not(inner))
    def _():
        core()
        edges()

    up_face().wait_send()
    down_face().wait_send()

    @pl.when(member < 2)
    def _():
        pass_up().wait_send()

    @pl.when(member >= 2)
    def _():
        pass_down().wait_send()

    @pl.when(last_dev)
    def _():
        for copy in seam_copies():
            copy.wait_send()

    for chunk in range(chunks):
        @pl.when(member > 0)
        def _():
            to_before(chunk).wait_send()

        @pl.when(member < TEAM - 1)
        def _():
            to_after(chunk).wait_send()


def on_device(populations, solidity, home_count):
    f32 = jnp.float32
    populations = populations.transpose(1, 0, 2).reshape(Q, HS, TILES, LANES).transpose(0, 2, 1, 3)
    populations = populations.reshape(Q, FIELD_ROWS, LANES)
    solidity = solidity.reshape(HS, TILES, LANES).transpose(1, 0, 2).reshape(-1, LANES)
    home_count = home_count.transpose(0, 2, 1)
    arguments = [pltpu.with_memory_space_constraint(a, pltpu.HBM) for a in (populations, solidity, home_count)]

    def boxes(places):
        return [pltpu.VMEM((places, AVG, FIELDS * depth, LANES), f32) for depth in DEPTH]

    def faces(*places):
        return pltpu.VMEM((*places, len(UP_FACE), PARTS, 8, LANES), f32)

    evolved = pl.pallas_call(
        kernel,
        out_shape=jax.ShapeDtypeStruct((Q * TILES * AVG, LANES), f32),
        in_specs=[pl.BlockSpec(memory_space=pltpu.HBM)] * 3,
        out_specs=pl.BlockSpec(memory_space=pltpu.VMEM),
        scratch_shapes=[
            pltpu.VMEM((FIELDS, FIELD_ROWS, LANES), f32),
            pltpu.VMEM((FIELDS, 2 * EDGE, LANES), f32),
            pltpu.SMEM(home_count.shape, jnp.int32),
            *boxes(2),
            *boxes(3),
            pltpu.VMEM((FIELDS, AVG + 1, HALVES, ROWS, LANES), f32),
            pltpu.VMEM((FIELDS, AVG + 1, HALVES, ROWS, LANES), f32),
            *[faces() for _ in range(3)],
            *[faces(2) for _ in range(2)],
            *[faces() for _ in range(2)],
            pltpu.VMEM((len(UP_FACE), 8, LANES), f32),
            pltpu.SemaphoreType.DMA((7,)),
            pltpu.SemaphoreType.DMA((2, len(CHUNKS))),
            pltpu.SemaphoreType.DMA((2, len(CHUNKS))),
            pltpu.SemaphoreType.DMA((10,)),
            pltpu.SemaphoreType.DMA((10,)),
            pltpu.SemaphoreType.REGULAR((2,)),
        ],
        compiler_params=pltpu.CompilerParams(
            collective_id=0, has_side_effects=True, vmem_limit_bytes=48 * 1024 * 1024
        ),
        cost_estimate=pl.CostEstimate(flops=8_000_000, bytes_accessed=3_000_000, transcendentals=0),
    )(*arguments)
    return evolved.reshape(Q, TILES, AVG, LANES).transpose(2, 0, 1, 3).reshape(AVG, Q, C)


def solution(mesh):
    return jax.shard_map(
        on_device,
        mesh=mesh,
        in_specs=(P(("grp", "dev"), None, None), P(("grp", "dev"), None), P("grp", None, None)),
        out_specs=P(("grp", "dev"), None, None),
        check_vma=False,
    )
```
